128 devices in a mesh: section: 8 (over y, core), dp: 16 (over z, x).
Axes of the slice: x: 4, y: 4, z: 4, core: 2. Of those that a mesh axis runs over, the one named last changes fastest.
Arguments:
- hidden: bfloat16 [4, 576, 8192], P(None, 'dp'), may hold values from -6 to 6
- lengths: int32 [4, 16], replicated, may hold values from 1 to 36, 256 in all within a row
- response_mask: int32 [4, 576], replicated, may hold values 0 or 1
- norm_gain: float32 [8, 8192], P('section'), may hold values from 0.25 to 1.75
- weight_in: bfloat16 [8, 8192, 256], P('section'), may hold values from -0.0625 to 0.0625
- weight_out: bfloat16 [8, 256, 8192], P('section'), may hold values from -0.375 to 0.375
- final_gain: float32 [8192], replicated, may hold values from 0.25 to 1.75
- value_heads: float32 [3, 8192], replicated, may hold values from -0.0625 to 0.0625
- old_values: float32 [3, 4, 576], replicated, may hold values from -6 to 6
- advantages: float32 [3, 4, 576], replicated, may hold values from -6 to 6
- multipliers: float32 [2], replicated, may hold values from 0.5 to 4
Outputs:
- grad_in: float32 [8, 8192, 256], P('section', 'dp')
- grad_out: float32 [8, 256, 8192], P('section', None, 'dp')
- objective: float32 [], replicated
The draws below stay inside these ranges and needn't reach their ends.
Inputs may be any that keep to these rules, and one draw needn't show every extreme that they name: In every micro-batch the 16 lengths sum to 256 and the longest equals 36.
All inputs are finite; a program needn't handle non-finite values.
Results may differ from the reference program's by a relative error of at most 0.034.
Values may be sent and summed in bfloat16 or wider, within the bound.
A program may use at most 128 MiB of HBM per device.

```python
import math
import jax
import jax.numpy as jnp
import numpy as np
from jax import lax

D = 8192
ADAPT = 256
HEADS = 3
MICRO = 4
CAP = 36
TOTAL = 256
ROWS = 576
LAYERS = 8
N_DP = 16


def place_ends(drawn, rng, smallest, largest):
    longest = drawn.shape.index(max(drawn.shape))
    spots = []
    for shift in (0, 1):
        where = [jax.random.randint(jax.random.fold_in(rng, axis), (), 0, length) for axis, length in enumerate(drawn.shape)]
        where[longest] = (where[longest] + shift) % drawn.shape[longest]
        spots.append(tuple(where))
    return drawn.at[spots[0]].set(smallest).at[spots[1]].set(largest)


def block_levels(stream_key, shape, pieces, smallest, high):
    gain = 1.0
    for dim, parts in pieces:
        steps = jax.random.uniform(jax.random.fold_in(jax.random.fold_in(stream_key, 6), dim), (parts,), jnp.float32, smallest / len(pieces), high / len(pieces))
        gain = gain * jnp.repeat(jnp.exp(steps), shape[dim] // parts).reshape((-1,) + (1,) * (len(shape) - 1 - dim))
    return gain


def profile(number_of, total, bound, skew):
    weights = [(1 << 20) // math.isqrt(rank ** skew) + 1 for rank in range(2, number_of + 1)]
    rest, holding = total - bound - (number_of - 1), [1] * (number_of - 1)
    while rest > 0:
        free = [i for i in range(number_of - 1) if holding[i] < bound]
        pool, budget = sum([weights[i] for i in free]), rest
        for i in free:
            addition = min(bound - holding[i], max(1, budget * weights[i] // pool), rest)
            holding[i] = holding[i] + addition
            rest = rest - addition
    return np.array([bound] + holding)


def uneven(key, number_of, total, limit, lean):
    if number_of == 2:
        one = jax.random.randint(key, (), max(1, total - limit), min(limit, total - 1) + 1)
        return jnp.stack([one, total - one])
    sizes = jnp.asarray(profile(number_of, total, limit, lean), jnp.int32)
    pairs = (number_of - 1) // 2
    donor, taker = sizes[1:1 + 2 * pairs:2], sizes[2:2 + 2 * pairs:2]
    room = jnp.minimum(donor - 1, limit - taker)
    moved = jax.random.randint(jax.random.fold_in(key, 1), (pairs,), 0, 1 << 20) % (room + 1)
    sizes = sizes.at[1:1 + 2 * pairs:2].set(donor - moved).at[2:2 + 2 * pairs:2].set(taker + moved)
    return sizes[jax.random.permutation(jax.random.fold_in(key, 2), number_of)]


def scatter_about(own_key, dims, deviation, bound, shards=(), kind=jnp.bfloat16):
    factor_of = block_levels(own_key, dims, shards, -0.22, 0.18) if shards else 1.0
    drawn = jax.random.normal(own_key, dims, jnp.float32) * deviation * factor_of
    return jnp.minimum(jnp.maximum(drawn, -bound), bound).astype(kind)


def setup_inputs(seed: int = 0) -> dict:
    key_of = jax.random.split(jax.random.key(seed), 12)
    return {
        "hidden": scatter_about(key_of[0], (MICRO, ROWS, D), 1.0, 6.0, ((1, 16),)),
        "lengths": jax.vmap(lambda own: uneven(own, N_DP, TOTAL, CAP, 2))(jax.random.split(key_of[1], MICRO)).reshape((MICRO, N_DP)).astype(jnp.int32),
        "response_mask": place_ends((jax.random.randint(key_of[2], (MICRO, ROWS), 0, 4) < 3).astype(jnp.int32), jax.random.fold_in(key_of[2], 1), 0, 1),
        "norm_gain": jnp.clip(1.0 + 0.15 * jax.random.normal(key_of[3], (LAYERS, D), jnp.float32), 0.25, 1.75),
        "weight_in": scatter_about(key_of[4], (LAYERS, D, ADAPT), D ** -0.5, 0.0625, ((0, 8),)),
        "weight_out": scatter_about(key_of[5], (LAYERS, ADAPT, D), ADAPT ** -0.5, 0.375, ((0, 8),)),
        "final_gain": jnp.clip(1.0 + 0.15 * jax.random.normal(key_of[6], (D,), jnp.float32), 0.25, 1.75),
        "value_heads": scatter_about(key_of[7], (HEADS, D), D ** -0.5, 0.0625, (), jnp.float32),
        "old_values": scatter_about(key_of[8], (HEADS, MICRO, ROWS), 1.0, 6.0, (), jnp.float32),
        "advantages": scatter_about(key_of[9], (HEADS, MICRO, ROWS), 1.0, 6.0, (), jnp.float32),
        "multipliers": jnp.clip(jnp.exp(jax.random.uniform(key_of[10], (2,), jnp.float32, math.log(0.5), math.log(4.0))), 0.5, 4.0),
    }


epsilon = 1e-05
loss_scale = 4096.0

def rms_factor(values):
    return lax.rsqrt(lax.optimization_barrier(jnp.mean(values * values, axis=-1, keepdims=True)) + epsilon)

def norm_backward(grad_normed, values, factor, scale):
    scaled = grad_normed * scale
    centred = lax.optimization_barrier(jnp.mean(scaled * values, axis=-1, keepdims=True))
    return factor * scaled - values * (factor * factor * factor) * centred

def layer_forward(block_in, norm_scale, matrix_in, matrix_out):
    values = block_in.astype(jnp.float32)
    factor = rms_factor(values)
    normed = (values * factor * norm_scale).astype(jnp.bfloat16)
    hidden_pre = jnp.dot(normed, matrix_in, preferred_element_type=jnp.float32)
    activated = (hidden_pre * jax.nn.sigmoid(hidden_pre)).astype(jnp.bfloat16)
    mixed = values + jnp.dot(activated, matrix_out, preferred_element_type=jnp.float32)
    return (mixed.astype(jnp.bfloat16), hidden_pre)

def layer_backward(block_in, hidden_pre, grad_rows, norm_scale, matrix_in, matrix_out):
    values = block_in.astype(jnp.float32)
    factor = rms_factor(values)
    normed = (values * factor * norm_scale).astype(jnp.bfloat16)
    sigmoid_pre = jax.nn.sigmoid(hidden_pre)
    activated = (hidden_pre * sigmoid_pre).astype(jnp.bfloat16)
    grad_act = lax.dot_general(grad_rows, matrix_out, (((1,), (1,)), ((), ())), preferred_element_type=jnp.float32)
    grad_matrix_out = lax.dot_general(activated, grad_rows, (((0,), (0,)), ((), ())), preferred_element_type=jnp.float32)
    grad_pre = (grad_act * sigmoid_pre * (1.0 + hidden_pre * (1.0 - sigmoid_pre))).astype(jnp.bfloat16)
    grad_matrix_in = lax.dot_general(normed, grad_pre, (((0,), (0,)), ((), ())), preferred_element_type=jnp.float32)
    grad_normed = lax.dot_general(grad_pre, matrix_in, (((1,), (1,)), ((), ())), preferred_element_type=jnp.float32)
    grad_block = grad_rows.astype(jnp.float32) + norm_backward(grad_normed, values, factor, norm_scale)
    return (grad_block.astype(jnp.bfloat16), grad_matrix_in, grad_matrix_out)

def head_gradient(block_out, final_gain, value_heads, targets, weights, coefficients, grad_scale):
    values = block_out.astype(jnp.float32)
    factor = rms_factor(values)
    normed = values * factor * final_gain
    estimates = lax.dot_general(value_heads, normed, (((1,), (1,)), ((), ())), precision=lax.Precision.HIGHEST, preferred_element_type=jnp.float32)
    errors = estimates - targets
    weighted = coefficients[:, None] * weights[None, :] * errors
    loss_part = 0.5 * jnp.sum(weighted * errors)
    grad_normed = lax.dot_general(weighted * grad_scale, value_heads, (((0,), (0,)), ((), ())), precision=lax.Precision.HIGHEST, preferred_element_type=jnp.float32)
    start_grad = norm_backward(grad_normed, values, factor, final_gain).astype(jnp.bfloat16)
    return (loss_part, start_grad)

def valid_index(lengths_row):
    ends_at = jnp.cumsum(lengths_row).astype(jnp.int32)
    position = jnp.arange(TOTAL, dtype=jnp.int32)
    passed = position[:, None] >= ends_at[None, :]
    shard_of = lax.optimization_barrier(jnp.sum(passed.astype(jnp.int32), axis=1)).astype(jnp.int32)
    before = lax.optimization_barrier(jnp.sum(jnp.where(passed, lengths_row[None, :], 0), axis=1)).astype(jnp.int32)
    return (shard_of * CAP + position - before).astype(jnp.int32)

def reference(hidden, lengths, response_mask, norm_gain, weight_in, weight_out, final_gain, value_heads, old_values, advantages, multipliers):
    coefficients = jnp.concatenate([jnp.ones((1,), jnp.float32), multipliers.astype(jnp.float32)])
    token_count = MICRO * TOTAL
    grad_scale = loss_scale / token_count
    targets_all = jnp.moveaxis(old_values + advantages, 1, 0)

    def one_micro(carried, micro_batch):
        grad_in_sum, grad_out_sum, loss_sum = carried
        block_hidden, lengths_row, mask_row, target_row = micro_batch
        chosen = valid_index(lengths_row)
        block_rows = jnp.take(block_hidden, chosen, axis=0)
        weights = jnp.take(mask_row, chosen).astype(jnp.float32)
        targets = jnp.take(target_row, chosen, axis=1)
        inputs_kept = []
        pre_kept = []
        for layer_index in range(LAYERS):
            inputs_kept.append(block_rows)
            block_rows, hidden_pre = layer_forward(block_rows, norm_gain[layer_index], weight_in[layer_index], weight_out[layer_index])
            pre_kept.append(hidden_pre)
        loss_part, grad_rows = head_gradient(block_rows, final_gain, value_heads, targets, weights, coefficients, grad_scale)
        for layer_index in reversed(range(LAYERS)):
            grad_rows, grad_matrix_in, grad_matrix_out = layer_backward(inputs_kept[layer_index], pre_kept[layer_index], grad_rows, norm_gain[layer_index], weight_in[layer_index], weight_out[layer_index])
            grad_in_sum = grad_in_sum.at[layer_index].add(grad_matrix_in)
            grad_out_sum = grad_out_sum.at[layer_index].add(grad_matrix_out)
        return ((grad_in_sum, grad_out_sum, loss_sum + loss_part), None)
    initial = (jnp.zeros((LAYERS, D, ADAPT), jnp.float32), jnp.zeros((LAYERS, ADAPT, D), jnp.float32), jnp.zeros((), jnp.float32))
    finished, ignored = lax.scan(one_micro, initial, (hidden, lengths, response_mask, targets_all))
    grad_in_sum, grad_out_sum, loss_sum = finished
    return (grad_in_sum, grad_out_sum, loss_sum / token_count)
```

```python
import functools

import jax
import jax.numpy as jnp
from jax import lax
from jax.experimental import pallas as pl
from jax.experimental.pallas import tpu as pltpu
from jax.sharding import PartitionSpec as P

EPS = 1e-05
LOSS_SCALE = 4096.0
BAL = 16

f32 = jnp.float32
bf16 = jnp.bfloat16
NT = (((1,), (1,)), ((), ()))
TN = (((0,), (0,)), ((), ()))


def mm(a, b, dims=(((1,), (0,)), ((), ()))):
    return lax.dot_general(a, b, dims, preferred_element_type=f32)


def exact(a, b, dims):
    return lax.dot_general(
        a, b, dims, precision=lax.Precision.HIGHEST, preferred_element_type=f32
    )


def split(v, terms):
    out = []
    for _ in range(terms):
        hi = v.astype(bf16)
        out.append(hi)
        v = v - hi.astype(f32)
    return out


def recurrence(layers, width, grad_scale, tiles_ref, rows_ref, side_ref, heads_ref, out_ref, held, sems):
    copies = {}
    for j in range(layers):
        for at in [(k, j) for k in range(j, layers)] + [(j, k) for k in range(j + 1, layers)]:
            copies[at] = pltpu.make_async_copy(
                tiles_ref.at[at[0], :, at[1]], held.at[at[0], at[1]], sems.at[at[0], at[1]]
            )
            copies[at].start()
    adapt = rows_ref.shape[2] // 2
    heads = heads_ref.shape[1]
    tile = lambda k, j: held[k, j].reshape(adapt, adapt)
    side = side_ref[...]
    sq = side[:, 0:1]
    est = [side[:, 1 + k : 2 + k] for k in range(heads)]
    mask = side[:, 4:5]
    target = [side[:, 5 + k : 6 + k] for k in range(heads)]
    coef = [side[:, 8 + k : 9 + k] for k in range(heads)]
    into = [rows_ref[k, :, :adapt] for k in range(layers)]
    onto = [rows_ref[k, :, adapt:] for k in range(layers)]
    pre, fac, kept = [], [], {}
    for j in range(layers):
        for k in range(j, layers):
            copies[k, j].wait()
            if k > j:
                copies[j, k].wait()
        f = lax.rsqrt(jnp.maximum(sq, 0.0) / width + EPS)
        p = f * into[j]
        sg = jax.nn.sigmoid(p)
        act = (p * sg).astype(bf16)
        out_ref[:, j * adapt : (j + 1) * adapt] = act.astype(f32)
        wide = act.astype(f32)
        pre.append(p)
        fac.append(f)
        for k in range(j):
            kept[j, k] = onto[k]
        before = onto[j]
        for k in range(layers):
            if k <= j:
                onto[k] = onto[k] + mm(act, tile(k, j))
            else:
                into[k] = into[k] + mm(act, tile(k, j))
                onto[k] = onto[k] + mm(act, tile(j, k), NT)
        sq = sq + jnp.sum(wide * (before + onto[j]), axis=1, keepdims=True)
        for k in range(heads):
            est[k] = est[k] + jnp.sum(wide * heads_ref[j, k : k + 1, :], axis=1, keepdims=True)
    f = lax.rsqrt(jnp.maximum(sq, 0.0) / width + EPS)
    loss = jnp.zeros_like(sq)
    along = jnp.zeros_like(sq)
    lane = lax.broadcasted_iota(jnp.int32, (side.shape[0], 128), 1)
    extra = jnp.zeros(lane.shape, f32)
    grads = []
    for k in range(heads):
        e = f * est[k]
        err = e - target[k]
        weighted = coef[k] * mask * err
        loss = loss + 0.5 * weighted * err
        scaled = weighted * grad_scale
        along = along + scaled * e
        grads.append(f * scaled)
        extra = jnp.where(lane == layers + k, grads[k], extra)
    extra = jnp.where(lane == layers + heads, loss, extra)
    total = f * f * along / width
    back = []
    for k in range(layers):
        start = -total * onto[k]
        for h in range(heads):
            start = start + grads[h] * heads_ref[k, h : h + 1, :]
        back.append(start)
    for l in range(layers - 1, -1, -1):
        extra = jnp.where(lane == l, total, extra)
        sg = jax.nn.sigmoid(pre[l])
        delta = (fac[l] * (back[l] * sg * (1.0 + pre[l] * (1.0 - sg)))).astype(bf16)
        wide = delta.astype(f32)
        out_ref[:, (layers + l) * adapt : (layers + l + 1) * adapt] = wide
        s = fac[l] / width * jnp.sum(wide * pre[l], axis=1, keepdims=True)
        total = total + s
        for k in range(l):
            back[k] = back[k] + mm(delta, tile(l, k), NT) - s * kept[l, k]
    out_ref[:, 2 * layers * adapt :] = extra


def local(
    hidden,
    lengths,
    response_mask,
    norm_gain,
    weight_in,
    weight_out,
    final_gain,
    value_heads,
    old_values,
    advantages,
    multipliers,
):
    shards = lax.axis_size("dp")
    layers = lax.axis_size("section")
    d = lax.axis_index("dp")
    l = lax.axis_index("section")
    micro, cap, width = hidden.shape
    heads = value_heads.shape[0]
    adapt = weight_in.shape[2]
    total = micro * BAL * shards
    part = width // shards
    own = total // (shards * layers)
    per_micro = total // micro

    gain = norm_gain[0]
    gw = (gain[:, None] * weight_in[0].astype(f32)).astype(bf16)
    wo = weight_out[0]
    wo_sl = lax.dynamic_slice(wo, (0, d * part), (adapt, part))
    gw_sl = lax.dynamic_slice(gw, (d * part, 0), (part, adapt))
    wo_all = lax.all_gather(wo_sl, "section")
    gw_all = lax.all_gather(gw_sl, "section")

    t_in = lax.dot_general(wo_all, gw_sl, (((2,), (0,)), ((), ())), preferred_element_type=f32)
    t_out = lax.dot_general(wo_all, wo_sl, (((2,), (1,)), ((), ())), preferred_element_type=f32)
    tiles = jnp.where(jnp.arange(layers)[:, None, None] < l, t_in, t_out).astype(bf16)
    tiles = lax.psum_scatter(tiles, "dp", scatter_dimension=1, tiled=True)
    tiles = lax.all_gather(tiles, ("section", "dp"))
    tiles = tiles.reshape(layers, shards, layers, adapt // shards, adapt)

    x0 = hidden.reshape(micro * cap, width)
    gfh = final_gain * value_heads
    x0f = x0.astype(f32)
    sq = jnp.sum(x0f * x0f, axis=1, keepdims=True)
    est = exact(x0f, gfh, NT)
    head_out = lax.all_gather(exact(gfh, wo.astype(f32), NT), "section")
    side = split(jnp.concatenate([sq, est], axis=1), 2)
    rows = jnp.concatenate(
        [mm(x0, gw).astype(bf16), mm(x0, wo, NT).astype(bf16)]
        + side
        + [jnp.zeros((micro * cap, 128 - 2 * (1 + heads)), bf16)],
        axis=1,
    )
    ends = jnp.cumsum(lengths, axis=1)
    begins = ends - lengths
    offsets = jnp.arange(cap, dtype=jnp.int32)
    base = (jnp.arange(micro, dtype=jnp.int32) * per_micro)[:, None, None]
    token = jnp.where(
        offsets[None, None, :] < lengths[:, :, None],
        begins[:, :, None] + offsets[None, None, :],
        -1,
    )
    mine = lax.dynamic_index_in_dim(token, d, 1, keepdims=False)
    mine = jnp.where(mine >= 0, mine + base[:, 0], -1).reshape(-1)
    place = (mine // own) % shards * (own * layers) + mine // (own * shards) * own + mine % own
    place = jnp.where(mine >= 0, place, -1)
    onehot = (jnp.arange(total, dtype=jnp.int32)[:, None] == place[None, :]).astype(bf16)
    rows = mm(onehot, rows).astype(bf16)
    rows = lax.psum_scatter(rows, "dp", scatter_dimension=0, tiled=True)
    rows = lax.all_to_all(
        rows.reshape(layers, own, rows.shape[1]), "section", split_axis=0, concat_axis=0
    )
    sides = rows[0, :, 2 * adapt :].astype(f32)
    rows = rows[:, :, : 2 * adapt].astype(f32)
    count = 1 + heads
    sides = sides[:, :count] + sides[:, count : 2 * count]

    first = (l * shards + d) * own
    batch = first // per_micro
    ids = first % per_micro + jnp.arange(own, dtype=jnp.int32)
    slot = lax.dynamic_index_in_dim(token, batch, 0, keepdims=False).reshape(-1)
    pick = (ids[:, None] == slot[None, :]).astype(f32)
    used = lax.dynamic_index_in_dim(response_mask, batch, 0, keepdims=False).astype(f32)
    aims = lax.dynamic_index_in_dim(old_values + advantages, batch, 1, keepdims=False)
    mask = jnp.sum(pick * used[None, :], axis=1, keepdims=True)
    aim = jnp.sum(pick[:, None, :] * aims[None], axis=2)
    coef = jnp.concatenate([jnp.ones((1,), f32), multipliers])
    side = jnp.concatenate(
        [
            sides,
            mask,
            aim,
            jnp.broadcast_to(coef[None], (own, heads)),
            jnp.zeros((own, 128 - 2 - 3 * heads), f32),
        ],
        axis=1,
    )

    vm = pl.BlockSpec(memory_space=pltpu.VMEM)
    state = pl.pallas_call(
        functools.partial(recurrence, layers, float(width), LOSS_SCALE / total),
        out_shape=jax.ShapeDtypeStruct((own, 2 * layers * adapt + 128), f32),
        in_specs=[pl.BlockSpec(memory_space=pl.ANY), vm, vm, vm],
        out_specs=vm,
        scratch_shapes=[
            pltpu.VMEM((layers, layers, shards, adapt // shards, adapt), bf16),
            pltpu.SemaphoreType.DMA((layers, layers)),
        ],
        compiler_params=pltpu.CompilerParams(vmem_limit_bytes=48 * 1024 * 1024),
        cost_estimate=pl.CostEstimate(
            flops=2 * own * adapt * adapt * 128, bytes_accessed=2 * 64 * adapt * adapt, transcendentals=0
        ),
        name="recurrence",
    )(tiles, rows, side, head_out)

    body = state[:, : 2 * layers * adapt].astype(bf16)
    scal = split(state[:, 2 * layers * adapt : 2 * layers * adapt + 16], 3)
    body = jnp.concatenate([body] + scal + [jnp.zeros((own, 80), bf16)], axis=1)
    body = lax.all_gather(body, ("section", "dp"), axis=0, tiled=True)
    scal = body[:, 2 * layers * adapt :].astype(f32)
    scal = scal[:, :16] + scal[:, 16:32] + scal[:, 32:48]

    x = lax.all_to_all(
        x0.reshape(micro * cap, shards, part), "dp", split_axis=1, concat_axis=0
    ).reshape(shards, micro, cap, part)
    x = jnp.swapaxes(x, 0, 1).reshape(micro, shards * cap, part)
    sel = jnp.arange(per_micro, dtype=jnp.int32)[None, :, None] == token.reshape(micro, 1, -1)
    x = lax.dot_general(
        sel.astype(bf16), x, (((2,), (1,)), ((0,), (0,))), preferred_element_type=f32
    )
    x = x.astype(bf16).reshape(total, part)

    acts = body[:, : layers * adapt]
    deltas = body[:, layers * adapt : 2 * layers * adapt]
    act = lax.dynamic_slice(acts, (0, l * adapt), (total, adapt))
    delta = lax.dynamic_slice(deltas, (0, l * adapt), (total, adapt))
    sigma = scal[:, :layers]
    ids = jnp.arange(layers)
    sig_l = jnp.sum(jnp.where(ids[None] == l, sigma, 0.0), axis=1, keepdims=True)
    by = jnp.where(ids[None] <= l, sig_l, sigma)
    by = jnp.repeat(-by, adapt, axis=1)
    later = jnp.repeat((ids > l).astype(bf16), adapt)
    earlier = jnp.repeat((ids < l).astype(f32), adapt)
    t_a = mm(act, (acts.astype(f32) * by).astype(bf16), TN).astype(bf16)
    t_d = (mm(act, deltas, TN).astype(bf16)) * later[None]
    grad_out = mm(t_a, wo_all.reshape(layers * adapt, part))
    grad_out += lax.dot_general(
        t_d.reshape(adapt, layers, adapt),
        gw_all,
        (((1, 2), (0, 2)), ((), ())),
        preferred_element_type=f32,
    )
    gfh_sl = lax.dynamic_slice(gfh, (0, d * part), (heads, part))
    t_h = exact(act.astype(f32), scal[:, layers : layers + heads], TN)
    grad_out += exact(t_h, gfh_sl, (((1,), (0,)), ((), ())))
    grad_out -= mm((act.astype(f32) * sig_l).astype(bf16), x, TN)
    t_i = (mm(acts, delta, TN) * earlier[:, None]).astype(bf16)
    grad_in = mm(x, delta, TN) + mm(wo_all.reshape(layers * adapt, part), t_i, TN)
    grad_in = lax.dynamic_slice(gain, (d * part,), (part,))[:, None] * grad_in
    objective = jnp.sum(scal[:, layers + heads]) / total
    return (grad_in[None], grad_out[None], objective)


def solution(mesh):
    return jax.shard_map(
        local,
        mesh=mesh,
        in_specs=(
            P(None, "dp", None),
            P(),
            P(),
            P("section", None),
            P("section", None, None),
            P("section", None, None),
            P(),
            P(),
            P(),
            P(),
            P(),
        ),
        out_specs=(P("section", "dp", None), P("section", None, "dp"), P()),
        check_vma=False,
    )
```

```python
import functools

import jax
import jax.numpy as jnp
from jax import lax
from jax.experimental import pallas as pl
from jax.experimental.pallas import tpu as pltpu
from jax.sharding import PartitionSpec as P

EPS = 1e-05
LOSS_SCALE = 4096.0
BAL = 16

f32 = jnp.float32
bf16 = jnp.bfloat16
NT = (((1,), (1,)), ((), ()))
TN = (((0,), (0,)), ((), ()))
NN = (((1,), (0,)), ((), ()))
MESH = pl.DeviceIdType.MESH
SIDE = 4
COPIES = 288


def mm(a, b, dims=NN):
    return lax.dot_general(a, b, dims, preferred_element_type=f32)


def exact(a, b, dims):
    return lax.dot_general(
        a, b, dims, precision=lax.Precision.HIGHEST, preferred_element_type=f32
    )


def split(v, terms):
    out = []
    for _ in range(terms):
        hi = v.astype(bf16)
        out.append(hi)
        v = v - hi.astype(f32)
    return out

def kernel(
    layers,
    width,
    grad_scale,
    wo_ref,
    gw_ref,
    x0_ref,
    rb_ref,
    sel_ref,
    hw_ref,
    side_ref,
    wo_out,
    gw_out,
    x_out,
    pay_out,
    wo_all,
    tp,
    r1,
    s1,
    r2,
    held,
    rr,
    sb,
    rq,
    mine,
    other,
    block,
    send_sem,
    recv_sem,
    local_sem,
):
    s = lax.axis_index("section")
    d = lax.axis_index("dp")
    y, c = s // 2, s % 2
    z, x = d // SIDE, d % SIDE
    me = {"x": x, "y": y, "z": z}
    shards = SIDE * SIDE
    adapt = hw_ref.shape[1]
    part = wo_ref.shape[1]
    heads = 3
    step = lambda a, off: (me[a] + off + SIDE) % SIDE

    def peer(axis, off):
        if axis == "x":
            return {"section": s, "dp": z * SIDE + step("x", off)}
        if axis == "z":
            return {"section": s, "dp": step("z", off) * SIDE + x}
        return {"section": step("y", off) * 2 + c, "dp": d}

    twin = {"section": y * 2 + (1 - c), "dp": d}

    def shard_at(off):
        return (d + off + shards) % shards

    def layer_at(off):
        return (s + off + layers) % layers

    barrier = pltpu.get_barrier_semaphore()
    for off in range(1, shards):
        pl.semaphore_signal(
            barrier, inc=1, device_id={"section": s, "dp": shard_at(off)}, device_id_type=MESH
        )
    for off in range(1, layers):
        pl.semaphore_signal(
            barrier, inc=1, device_id={"section": layer_at(off), "dp": d}, device_id_type=MESH
        )
    pl.semaphore_wait(barrier, shards + layers - 2)

    issued = []
    count = [0, 0]

    def new():
        count[0] += 1
        return count[0] - 1

    def remote(src, dst, at, to):
        return pltpu.make_async_remote_copy(
            src_ref=src,
            dst_ref=dst,
            send_sem=send_sem.at[at],
            recv_sem=recv_sem.at[at],
            device_id=to,
            device_id_type=MESH,
        )

    def send(src, dst, at, to):
        copy = remote(src, dst, at, to)
        copy.start()
        issued.append(copy)

    def arrived(dst, at):
        remote(dst, dst, at, twin).wait_recv()

    def local(src, dst):
        count[1] += 1
        copy = pltpu.make_async_copy(src, dst, local_sem.at[count[1] - 1])
        copy.start()
        return copy

    class Ring:
        def __init__(self, axis, slab, swaps=False):
            self.slab = slab
            self.ids = [new() for _ in range(6)]
            self.plus, self.minus = peer(axis, 1), peer(axis, -1)
            self.swaps = {}
            if swaps:
                for v in (0, -1, 1, 2):
                    for h in (0, 1):
                        self.swaps[v, h] = new()

        def send(self, v, h, n, to):
            ref = self.slab(v, h, c)
            send(ref, ref, self.ids[n], to)

        def wait(self, v, h, n):
            arrived(self.slab(v, h, c), self.ids[n])
            self.swap(v, h)

        def swap(self, v, h):
            if self.swaps:
                ref = self.slab(v, h, c)
                send(ref, ref, self.swaps[v, h], twin)

        def start(self):
            self.send(0, 0, 0, self.plus)
            self.send(0, 1, 2, self.minus)
            self.send(0, 1, 1, self.plus)
            self.send(0, 0, 3, self.minus)
            self.swap(0, 0)
            self.swap(0, 1)

        def relay(self):
            arrived(self.slab(-1, 0, c), self.ids[0])
            self.send(-1, 0, 4, self.plus)
            arrived(self.slab(1, 1, c), self.ids[2])
            self.send(1, 1, 5, self.minus)
            self.swap(-1, 0)
            self.swap(1, 1)

        def finish(self):
            self.wait(-1, 1, 1)
            self.wait(1, 0, 3)
            self.wait(2, 0, 4)
            self.wait(2, 1, 5)

        def twins(self):
            for (v, h), at in self.swaps.items():
                arrived(self.slab(v, h, 1 - c), at)

    def gather(at, columns):
        third = (columns // 384) * 128
        bounds = [0, third, 2 * third, columns]
        orders = [("x", "z", "y"), ("z", "y", "x"), ("y", "x", "z")]
        for phase in range(3):
            rings = []
            for p, order in enumerate(orders):
                lo, hi = bounds[p], bounds[p + 1]
                mid = lo + ((hi - lo) // 256) * 128
                cuts = [(lo, mid - lo), (mid, hi - mid)]

                def slab(v, h, core, order=order, cuts=cuts):
                    where = dict(me)
                    for a in order[:phase]:
                        where[a] = pl.ds(0, SIDE)
                    where[order[phase]] = step(order[phase], v)
                    return at(where, core, pl.ds(*cuts[h]))

                rings.append(Ring(order[phase], slab, swaps=phase == 2))
            for ring in rings:
                ring.start()
            for ring in rings:
                ring.relay()
            for ring in rings:
                ring.finish()
        for ring in rings:
            ring.twins()

    half = wo_ref.shape[0] // 2
    wo_ring = Ring(
        "y", lambda v, h, core: wo_all.at[step("y", v), core, pl.ds(h * half, half)], True
    )
    wo_all[y, c] = wo_ref[...]
    wo_ring.start()
    wide = part // 2
    keep = []
    for h in (0, 1):
        keep.append(
            local(
                x0_ref.at[:, pl.ds(pl.multiple_of(d * part + h * wide, wide), wide)],
                x_out.at[h, d],
            )
        )
    x_ids = [new() for _ in range(shards)]
    x_swaps = [new() for _ in range(shards)]
    for off in range(1, shards):
        to = shard_at(off)
        send(
            x0_ref.at[:, pl.ds(pl.multiple_of(to * part + c * wide, wide), wide)],
            x_out.at[c, d],
            x_ids[off],
            {"section": s, "dp": to},
        )
    long = gw_ref.shape[0] // 2
    gw_ring = Ring(
        "y", lambda v, h, core: gw_out.at[step("y", v), core, pl.ds(h * long, long)], True
    )
    own_gw = local(gw_ref, gw_out.at[y, c])

    row_ids = [new() for _ in range(shards)]
    for off in range(1, shards):
        to = shard_at(off)
        send(rb_ref.at[to], rr.at[d], row_ids[off], {"section": s, "dp": to})
    rr[d] = rb_ref[d]

    wo_ring.relay()
    wo_ring.finish()
    wo_ring.twins()
    own_gw.wait()
    gw_ring.start()
    keep.append(local(wo_all, wo_out))

    for j in range(layers):
        rhs = jnp.where(j < s, gw_ref[...], wo_ref[...].T)
        tile = mm(wo_all[j // 2, j % 2], rhs).astype(bf16)
        tp[:, :, :, j * adapt : (j + 1) * adapt] = tile.reshape(SIDE, SIDE, shards, adapt)

    mid = layers * adapt // 2
    first = {}
    for off in (2, 1, 3):
        for n, axis in enumerate(("x", "z")):
            first[n, off] = new()
            to = step(axis, off)
            cut = pl.ds(n * mid, mid)
            src = tp.at[:, to, :, cut] if n == 0 else tp.at[to, :, :, cut]
            send(src, r1.at[n, off - 1], first[n, off], peer(axis, off))
    for off in range(1, shards):
        arrived(rr.at[shard_at(-off)], row_ids[off])
    tokens = mm(sel_ref[...], rr[...].reshape(shards * rr.shape[1], rr.shape[2]))
    own = tokens.shape[0] // layers
    for k in range(layers):
        sb[k, :own] = tokens[k * own : (k + 1) * own]
        sb[k, own : 2 * own, :adapt] = hw_ref[...]
        sb[k, own : 2 * own, adapt:] = jnp.zeros((own, sb.shape[2] - adapt), f32)
    token_ids = [new() for _ in range(layers)]
    for off in range(1, layers):
        to = layer_at(off)
        send(sb.at[to], rq.at[s], token_ids[off], {"section": to, "dp": d})
    rq[s] = sb[s]
    second = {}
    for n in (0, 1):
        kept = tp[:, x, :, :mid] if n == 0 else tp[z, :, :, mid:]
        kept = kept.astype(f32)
        for off in (1, 3, 2):
            arrived(r1.at[n, off - 1], first[n, off])
            kept = kept + r1[n, off - 1].astype(f32)
        s1[n] = kept.astype(bf16)
        axis = ("z", "x")[n]
        for off in (2, 1, 3):
            second[n, off] = new()
            send(s1.at[n, step(axis, off)], r2.at[n, off - 1], second[n, off], peer(axis, off))
    gw_ring.relay()
    for n in (0, 1):
        kept = s1[n, me[("z", "x")[n]]].astype(f32)
        for off in (1, 3, 2):
            arrived(r2.at[n, off - 1], second[n, off])
            kept = kept + r2[n, off - 1].astype(f32)
        held[y, c, z, x, :, n * mid : (n + 1) * mid] = kept.astype(bf16)
    gather(lambda w, core, cut: held.at[w["y"], core, w["z"], w["x"], :, cut], layers * adapt)
    for off in range(1, layers):
        arrived(rq.at[layer_at(-off)], token_ids[off])
    for off in range(1, shards):
        src = x_out.at[c, shard_at(-off)]
        arrived(src, x_ids[off])
        send(src, src, x_swaps[off], twin)

    def tile(l, j):
        return held[l // 2, l % 2, :, :, :, j * adapt : (j + 1) * adapt].reshape(adapt, adapt)

    recurrence(layers, width, grad_scale, heads, tile, rq, side_ref, mine)
    swap = new()
    send(mine.at[1 - c], other, swap, twin)
    arrived(other, swap)
    a, b = mine[c], other[...]
    block[...] = jnp.concatenate([jnp.where(c == 0, a, b), jnp.where(c == 0, b, a)], axis=0).astype(
        bf16
    )
    local(block, pay_out.at[c, y, z, x]).wait()
    gather(lambda w, core, cut: pay_out.at[core, w["y"], w["z"], w["x"], :, cut], block.shape[1])
    gw_ring.finish()
    gw_ring.twins()
    for off in range(1, shards):
        arrived(x_out.at[1 - c, shard_at(-off)], x_swaps[off])
    for copy in keep:
        copy.wait()
    for copy in issued:
        copy.wait_send()


def recurrence(layers, width, grad_scale, heads, tile, rows_ref, side_ref, out_ref):
    adapt = 256
    own = side_ref.shape[0]
    sums = rows_ref[0, :own, 2 * adapt :]
    side = side_ref[...]
    part = lambda k: sums[:, k : k + 1] + sums[:, 1 + heads + k : 2 + heads + k]
    sq = part(0)
    est = [part(1 + k) for k in range(heads)]
    mask = side[:, 0:1]
    target = [side[:, 1 + k : 2 + k] for k in range(heads)]
    coef = [side[:, 4 + k : 5 + k] for k in range(heads)]
    into = [rows_ref[k, :own, :adapt] for k in range(layers)]
    onto = [rows_ref[k, :own, adapt : 2 * adapt] for k in range(layers)]
    head_out = [
        [rows_ref[k, own + h : own + h + 1, :adapt] for h in range(heads)] for k in range(layers)
    ]
    pre, fac, kept = [], [], {}
    for j in range(layers):
        f = lax.rsqrt(jnp.maximum(sq, 0.0) / width + EPS)
        p = f * into[j]
        act = (p * jax.nn.sigmoid(p)).astype(bf16)
        wide = act.astype(f32)
        out_ref[0, :, j * adapt : (j + 1) * adapt] = wide
        pre.append(p)
        fac.append(f)
        for k in range(j):
            kept[j, k] = onto[k]
        before = onto[j]
        for k in range(layers):
            if k <= j:
                onto[k] = onto[k] + mm(act, tile(k, j))
            else:
                into[k] = into[k] + mm(act, tile(k, j))
                onto[k] = onto[k] + mm(act, tile(j, k), NT)
        sq = sq + jnp.sum(wide * (before + onto[j]), axis=1, keepdims=True)
        for h in range(heads):
            est[h] = est[h] + jnp.sum(wide * head_out[j][h], axis=1, keepdims=True)
    f = lax.rsqrt(jnp.maximum(sq, 0.0) / width + EPS)
    loss = jnp.zeros_like(sq)
    along = jnp.zeros_like(sq)
    lane = lax.broadcasted_iota(jnp.int32, (own, 128), 1)
    extra = jnp.zeros(lane.shape, f32)
    grads = []
    for h in range(heads):
        e = f * est[h]
        err = e - target[h]
        weighted = coef[h] * mask * err
        loss = loss + 0.5 * weighted * err
        scaled = weighted * grad_scale
        along = along + scaled * e
        grads.append(f * scaled)
        extra = jnp.where(lane == layers + h, grads[h], extra)
    extra = jnp.where(lane == layers + heads, loss, extra)
    total = f * f * along / width
    back = []
    for k in range(layers):
        start = -total * onto[k]
        for h in range(heads):
            start = start + grads[h] * head_out[k][h]
        back.append(start)
    for l in range(layers - 1, -1, -1):
        extra = jnp.where(lane == l, total, extra)
        sg = jax.nn.sigmoid(pre[l])
        delta = (fac[l] * (back[l] * sg * (1.0 + pre[l] * (1.0 - sg)))).astype(bf16)
        wide = delta.astype(f32)
        out_ref[1, :, l * adapt : (l + 1) * adapt] = wide
        s = fac[l] / width * jnp.sum(wide * pre[l], axis=1, keepdims=True)
        total = total + s
        for k in range(l):
            back[k] = back[k] + mm(delta, tile(l, k), NT) - s * kept[l, k]
    high = extra.astype(bf16).astype(f32)
    out_ref[0, :, layers * adapt :] = high
    out_ref[1, :, layers * adapt :] = extra - high


def local(
    hidden,
    lengths,
    response_mask,
    norm_gain,
    weight_in,
    weight_out,
    final_gain,
    value_heads,
    old_values,
    advantages,
    multipliers,
):
    shards = lax.axis_size("dp")
    layers = lax.axis_size("section")
    d = lax.axis_index("dp")
    l = lax.axis_index("section")
    micro, cap, width = hidden.shape
    heads = value_heads.shape[0]
    adapt = weight_in.shape[2]
    total = micro * BAL * shards
    part = width // shards
    own = total // (shards * layers)
    per_micro = total // micro

    gain = norm_gain[0]
    gw = (gain[:, None] * weight_in[0].astype(f32)).astype(bf16)
    wo = weight_out[0]
    wo_sl = lax.dynamic_slice(wo, (0, d * part), (adapt, part))
    gw_sl = lax.dynamic_slice(gw, (d * part, 0), (part, adapt))

    x0 = hidden.reshape(micro * cap, width)
    gfh = final_gain * value_heads
    x0f = x0.astype(f32)
    sq = jnp.sum(x0f * x0f, axis=1, keepdims=True)
    est = exact(x0f, gfh, NT)
    head_out = exact(gfh, wo.astype(f32), NT)
    head_out = jnp.concatenate([head_out, jnp.zeros((own - heads, adapt), f32)], axis=0)
    side = split(jnp.concatenate([sq, est], axis=1), 2)
    rows = jnp.concatenate(
        [mm(x0, gw).astype(bf16), mm(x0, wo, NT).astype(bf16)]
        + side
        + [jnp.zeros((micro * cap, 128 - 2 * (1 + heads)), bf16)],
        axis=1,
    )
    ends = jnp.cumsum(lengths, axis=1)
    begins = ends - lengths
    offsets = jnp.arange(cap, dtype=jnp.int32)
    batches = jnp.arange(micro, dtype=jnp.int32)
    most = 3
    begin = jnp.take(begins, d, axis=1)[:, None]
    p = begin + offsets[None]
    n = p // shards - (begin - p % shards + shards - 1) // shards
    slot = (p % shards) * 16 + batches[:, None] * most + n
    slot = jnp.where(offsets[None] < jnp.take(lengths, d, axis=1)[:, None], slot, -1).reshape(-1)
    put = (jnp.arange(shards * 16, dtype=jnp.int32)[:, None] == slot[None]).astype(bf16)
    rows = mm(put, rows).astype(bf16).reshape(shards, 16, rows.shape[1])
    q = (begins - d + shards - 1) // shards
    p = d + shards * (q[:, :, None] + jnp.arange(most, dtype=jnp.int32))
    seat = (2 * batches[:, None, None] + p // 128) * own + (p // shards) % own
    seat = jnp.where(p < ends[:, :, None], seat, -1)
    seat = jnp.swapaxes(seat, 0, 1).reshape(shards, micro * most)
    seat = jnp.pad(seat, ((0, 0), (0, 16 - micro * most)), constant_values=-1).reshape(-1)
    sel = (jnp.arange(layers * own, dtype=jnp.int32)[:, None] == seat[None]).astype(bf16)

    token = jnp.where(
        offsets[None, None, :] < lengths[:, :, None],
        begins[:, :, None] + offsets[None, None, :],
        -1,
    )
    batch = l // 2
    ids = (l % 2) * 128 + shards * jnp.arange(own, dtype=jnp.int32) + d
    spot = lax.dynamic_index_in_dim(token, batch, 0, keepdims=False).reshape(-1)
    pick = (ids[:, None] == spot[None, :]).astype(f32)
    used = lax.dynamic_index_in_dim(response_mask, batch, 0, keepdims=False).astype(f32)
    aims = lax.dynamic_index_in_dim(old_values + advantages, batch, 1, keepdims=False)
    mask = jnp.sum(pick * used[None, :], axis=1, keepdims=True)
    aim = jnp.sum(pick[:, None, :] * aims[None], axis=2)
    coef = jnp.concatenate([jnp.ones((1,), f32), multipliers])
    side = jnp.concatenate(
        [
            mask,
            aim,
            jnp.broadcast_to(coef[None], (own, heads)),
            jnp.zeros((own, 127 - 2 * heads), f32),
        ],
        axis=1,
    )

    vm = pl.BlockSpec(memory_space=pltpu.VMEM)
    hbm = pl.BlockSpec(memory_space=pl.ANY)
    columns = layers * adapt + 128
    wo_all, gw_all, x, pay = pl.pallas_call(
        functools.partial(kernel, layers, float(width), LOSS_SCALE / total),
        out_shape=(
            jax.ShapeDtypeStruct((SIDE, 2, adapt, part), bf16),
            jax.ShapeDtypeStruct((SIDE, 2, part, adapt), bf16),
            jax.ShapeDtypeStruct((2, shards, micro * cap, part // 2), bf16),
            jax.ShapeDtypeStruct((2, SIDE, SIDE, SIDE, 16, columns), bf16),
        ),
        in_specs=[vm, vm, hbm, vm, vm, vm, vm],
        out_specs=(hbm, hbm, hbm, hbm),
        scratch_shapes=[
            pltpu.VMEM((SIDE, 2, adapt, part), bf16),
            pltpu.VMEM((SIDE, SIDE, 16, layers * adapt), bf16),
            pltpu.VMEM((2, 3, SIDE, 16, layers * adapt // 2), bf16),
            pltpu.VMEM((2, SIDE, 16, layers * adapt // 2), bf16),
            pltpu.VMEM((2, 3, 16, layers * adapt // 2), bf16),
            pltpu.VMEM((SIDE, 2, SIDE, SIDE, 16, layers * adapt), bf16),
            pltpu.VMEM((shards, 16, 2 * adapt + 128), bf16),
            pltpu.VMEM((layers, 2 * own, 2 * adapt + 128), f32),
            pltpu.VMEM((layers, 2 * own, 2 * adapt + 128), f32),
            pltpu.VMEM((2, own, columns), f32),
            pltpu.VMEM((own, columns), f32),
            pltpu.VMEM((16, columns), bf16),
            pltpu.SemaphoreType.DMA((COPIES,)),
            pltpu.SemaphoreType.DMA((COPIES,)),
            pltpu.SemaphoreType.DMA((8,)),
        ],
        compiler_params=pltpu.CompilerParams(
            vmem_limit_bytes=48 * 1024 * 1024, collective_id=0, has_side_effects=True
        ),
        cost_estimate=pl.CostEstimate(
            flops=10**9, bytes_accessed=3 * 10**7, transcendentals=0
        ),
        name="layers",
    )(wo_sl, gw_sl, x0, rows, sel, head_out, side)
    acts = pay[0].reshape(total, columns)
    deltas = pay[1].reshape(total, columns)
    scal = acts[:, layers * adapt :].astype(f32) + deltas[:, layers * adapt :].astype(f32)
    acts, deltas = acts[:, : layers * adapt], deltas[:, : layers * adapt]

    place = (batches[:, None, None] * shards + token % shards) * 16 + token // 128 * own
    place = jnp.where(token >= 0, place + token // shards % own, -1)
    place = jnp.swapaxes(place, 0, 1).reshape(1, -1)
    seat = (jnp.arange(total, dtype=jnp.int32)[:, None] == place).astype(bf16)
    x = x.reshape(2, shards * micro * cap, part // 2)
    x = jnp.concatenate([mm(seat, x[0]).astype(bf16), mm(seat, x[1]).astype(bf16)], axis=1)

    act = lax.dynamic_slice(acts, (0, l * adapt), (total, adapt))
    delta = lax.dynamic_slice(deltas, (0, l * adapt), (total, adapt))
    sigma = scal[:, :layers]
    ids = jnp.arange(layers)
    sig_l = jnp.sum(jnp.where(ids[None] == l, sigma, 0.0), axis=1, keepdims=True)
    by = jnp.where(ids[None] <= l, sig_l, sigma)
    by = jnp.repeat(-by, adapt, axis=1)
    later = jnp.repeat((ids > l).astype(bf16), adapt)
    earlier = jnp.repeat((ids < l).astype(f32), adapt)
    wo_all = wo_all.reshape(layers * adapt, part)
    gw_all = gw_all.reshape(layers, part, adapt)
    t_a = mm(act, (acts.astype(f32) * by).astype(bf16), TN).astype(bf16)
    t_d = (mm(act, deltas, TN).astype(bf16)) * later[None]
    grad_out = mm(t_a, wo_all)
    grad_out += lax.dot_general(
        t_d.reshape(adapt, layers, adapt),
        gw_all,
        (((1, 2), (0, 2)), ((), ())),
        preferred_element_type=f32,
    )
    gfh_sl = lax.dynamic_slice(gfh, (0, d * part), (heads, part))
    t_h = exact(act.astype(f32), scal[:, layers : layers + heads], TN)
    grad_out += exact(t_h, gfh_sl, NN)
    grad_out -= mm((act.astype(f32) * sig_l).astype(bf16), x, TN)
    t_i = (mm(acts, delta, TN) * earlier[:, None]).astype(bf16)
    grad_in = mm(x, delta, TN) + mm(wo_all, t_i, TN)
    grad_in = lax.dynamic_slice(gain, (d * part,), (part,))[:, None] * grad_in
    objective = jnp.sum(scal[:, layers + heads]) / total
    return (grad_in[None], grad_out[None], objective)


def solution(mesh):
    return jax.shard_map(
        local,
        mesh=mesh,
        in_specs=(
            P(None, "dp", None),
            P(),
            P(),
            P("section", None),
            P("section", None, None),
            P("section", None, None),
            P(),
            P(),
            P(),
            P(),
            P(),
        ),
        out_specs=(P("section", "dp", None), P("section", None, "dp"), P()),
        check_vma=False,
    )
```

```python
import functools

import jax
import jax.numpy as jnp
from jax import lax
from jax.experimental import pallas as pl
from jax.experimental.pallas import tpu as pltpu
from jax.sharding import PartitionSpec as P

EPS = 1e-05
LOSS_SCALE = 4096.0
BAL = 16

f32 = jnp.float32
bf16 = jnp.bfloat16
NT = (((1,), (1,)), ((), ()))
TN = (((0,), (0,)), ((), ()))
NN = (((1,), (0,)), ((), ()))
MESH = pl.DeviceIdType.MESH
SIDE = 4
COPIES = 288


def mm(a, b, dims=NN):
    return lax.dot_general(a, b, dims, preferred_element_type=f32)


def exact(a, b, dims):
    return lax.dot_general(
        a, b, dims, precision=lax.Precision.HIGHEST, preferred_element_type=f32
    )


def split(v, terms):
    out = []
    for _ in range(terms):
        hi = v.astype(bf16)
        out.append(hi)
        v = v - hi.astype(f32)
    return out

def kernel(
    layers,
    width,
    grad_scale,
    win_ref,
    wout_ref,
    gw_ref,
    gain_ref,
    x0_ref,
    put_ref,
    sel_ref,
    side_ref,
    place_ref,
    head_ref,
    scale_ref,
    grad_in_ref,
    grad_out_ref,
    loss_ref,
    win,
    wout,
    sums,
    wo_all,
    gw_all,
    x_all,
    x_sel,
    pay,
    rb,
    tp,
    r1,
    s1,
    r2,
    held,
    rr,
    sb,
    rq,
    mine,
    other,
    block,
    sums_t,
    send_sem,
    recv_sem,
    local_sem,
):
    s = lax.axis_index("section")
    d = lax.axis_index("dp")
    y, c = s // 2, s % 2
    z, x = d // SIDE, d % SIDE
    me = {"x": x, "y": y, "z": z}
    shards = SIDE * SIDE
    part, adapt = gw_ref.shape
    heads = 3
    rows = put_ref.shape[1]
    step = lambda a, off: (me[a] + off + SIDE) % SIDE

    def peer(axis, off):
        if axis == "x":
            return {"section": s, "dp": z * SIDE + step("x", off)}
        if axis == "z":
            return {"section": s, "dp": step("z", off) * SIDE + x}
        return {"section": step("y", off) * 2 + c, "dp": d}

    twin = {"section": y * 2 + (1 - c), "dp": d}

    def shard_at(off):
        return (d + off + shards) % shards

    def layer_at(off):
        return (s + off + layers) % layers

    barrier = pltpu.get_barrier_semaphore()
    for off in range(1, shards):
        pl.semaphore_signal(
            barrier, inc=1, device_id={"section": s, "dp": shard_at(off)}, device_id_type=MESH
        )
    for off in range(1, layers):
        pl.semaphore_signal(
            barrier, inc=1, device_id={"section": layer_at(off), "dp": d}, device_id_type=MESH
        )
    pl.semaphore_wait(barrier, shards + layers - 2)

    issued = []
    count = [0, 0]

    def new():
        count[0] += 1
        return count[0] - 1

    def remote(src, dst, at, to):
        return pltpu.make_async_remote_copy(
            src_ref=src,
            dst_ref=dst,
            send_sem=send_sem.at[at],
            recv_sem=recv_sem.at[at],
            device_id=to,
            device_id_type=MESH,
        )

    def send(src, dst, at, to):
        copy = remote(src, dst, at, to)
        copy.start()
        issued.append(copy)

    def arrived(dst, at):
        remote(dst, dst, at, twin).wait_recv()

    def local(src, dst):
        count[1] += 1
        copy = pltpu.make_async_copy(src, dst, local_sem.at[count[1] - 1])
        copy.start()
        return copy

    class Ring:
        def __init__(self, axis, slab, swaps=False):
            self.slab = slab
            self.ids = [new() for _ in range(6)]
            self.plus, self.minus = peer(axis, 1), peer(axis, -1)
            self.swaps = {}
            if swaps:
                for v in (0, -1, 1, 2):
                    for h in (0, 1):
                        self.swaps[v, h] = new()

        def send(self, v, h, n, to):
            ref = self.slab(v, h, c)
            send(ref, ref, self.ids[n], to)

        def wait(self, v, h, n):
            arrived(self.slab(v, h, c), self.ids[n])
            self.swap(v, h)

        def swap(self, v, h):
            if self.swaps:
                ref = self.slab(v, h, c)
                send(ref, ref, self.swaps[v, h], twin)

        def start(self):
            self.send(0, 0, 0, self.plus)
            self.send(0, 1, 2, self.minus)
            self.send(0, 1, 1, self.plus)
            self.send(0, 0, 3, self.minus)
            self.swap(0, 0)
            self.swap(0, 1)

        def relay(self):
            arrived(self.slab(-1, 0, c), self.ids[0])
            self.send(-1, 0, 4, self.plus)
            arrived(self.slab(1, 1, c), self.ids[2])
            self.send(1, 1, 5, self.minus)
            self.swap(-1, 0)
            self.swap(1, 1)

        def finish(self):
            self.wait(-1, 1, 1)
            self.wait(1, 0, 3)
            self.wait(2, 0, 4)
            self.wait(2, 1, 5)

        def twins(self):
            for (v, h), at in self.swaps.items():
                arrived(self.slab(v, h, 1 - c), at)

    def gather(at, columns, meanwhile=None):
        third = (columns // 384) * 128
        bounds = [0, third, 2 * third, columns]
        orders = [("x", "z", "y"), ("z", "y", "x"), ("y", "x", "z")]
        for phase in range(3):
            rings = []
            for p, order in enumerate(orders):
                lo, hi = bounds[p], bounds[p + 1]
                mid = lo + ((hi - lo) // 256) * 128
                cuts = [(lo, mid - lo), (mid, hi - mid)]

                def slab(v, h, core, order=order, cuts=cuts):
                    where = dict(me)
                    for a in order[:phase]:
                        where[a] = pl.ds(0, SIDE)
                    where[order[phase]] = step(order[phase], v)
                    return at(where, core, pl.ds(*cuts[h]))

                rings.append(Ring(order[phase], slab, swaps=phase == 2))
            for ring in rings:
                ring.start()
            if phase == 2 and meanwhile is not None:
                meanwhile()
            for ring in rings:
                ring.relay()
            for ring in rings:
                ring.finish()
        for ring in rings:
            ring.twins()

    chunks = win.shape[0]
    loads = []
    for k in range(chunks):
        loads.append(local(win_ref.at[pl.ds(k * part, part)], win.at[k]))
        loads.append(local(wout_ref.at[:, pl.ds(k * part, part)], wout.at[k]))

    half = adapt // 2
    wo_ring = Ring(
        "y", lambda v, h, core: wo_all.at[step("y", v), core, pl.ds(h * half, half)], True
    )
    columns = pl.ds(pl.multiple_of(d * part, part), part)
    local(wout_ref.at[:, columns], wo_all.at[y, c]).wait()
    wo_ring.start()
    wide = part // 2
    keep = []
    for h in (0, 1):
        keep.append(
            local(
                x0_ref.at[:rows, pl.ds(pl.multiple_of(d * part + h * wide, wide), wide)],
                x_all.at[h, d],
            )
        )
    x_ids = [new() for _ in range(shards)]
    x_swaps = [new() for _ in range(shards)]
    for off in range(1, shards):
        to = shard_at(off)
        send(
            x0_ref.at[:rows, pl.ds(pl.multiple_of(to * part + c * wide, wide), wide)],
            x_all.at[c, d],
            x_ids[off],
            {"section": s, "dp": to},
        )
    long = part // 2
    gw_ring = Ring(
        "y", lambda v, h, core: gw_all.at[step("y", v), core, pl.ds(h * long, long)], True
    )
    gw_all[y, c] = gw_ref[...]

    square = jnp.zeros((rows, 128), f32)
    for copy in loads:
        copy.wait()
    sums[...] = jnp.zeros(sums.shape, f32)

    def chunk(k, square):
        cut = pl.ds(pl.multiple_of(k * part, part), part)
        both = x0_ref[:, cut]
        x = both[:rows].astype(f32)
        for i in range(part // 128):
            piece = x[:, i * 128 : (i + 1) * 128]
            square = square + piece * piece
        gained = (x * gain_ref[:, cut]).astype(bf16)
        sums[:rows, :adapt] += mm(gained, win[k])
        sums[:, adapt : 2 * adapt] += mm(both, wout[k], NT)
        sums[:rows, 2 * adapt :] += mm(both[:rows], both[rows:], NT)
        return square

    square = jnp.sum(lax.fori_loop(0, chunks, chunk, square), axis=1, keepdims=True)
    heads_by = [rows + 3 * h for h in range(heads)]
    est = sums[:rows, 2 * adapt :]
    lane = lax.broadcasted_iota(jnp.int32, (rows, 128), 1)
    dots = [square]
    for h in range(heads):
        dots.append(est[:, 3 * h : 3 * h + 1] + est[:, 3 * h + 1 : 3 * h + 2] + est[:, 3 * h + 2 : 3 * h + 3])
    own_side = jnp.zeros((rows, 128), f32)
    for k, v in enumerate(dots):
        high = v.astype(bf16).astype(f32)
        own_side = jnp.where(lane == k, high, own_side)
        own_side = jnp.where(lane == len(dots) + k, v - high, own_side)
    ab = jnp.concatenate([sums[:rows, : 2 * adapt], own_side], axis=1).astype(bf16)
    rb[...] = mm(put_ref[...], ab).astype(bf16).reshape(rb.shape)

    row_ids = [new() for _ in range(shards)]
    for off in range(1, shards):
        to = shard_at(off)
        send(rb.at[to], rr.at[d], row_ids[off], {"section": s, "dp": to})
    rr[d] = rb[d]

    wo_ring.relay()
    wo_ring.finish()
    wo_ring.twins()
    gw_ring.start()

    wo_turned = wo_all[y, c].T
    for j in range(layers):
        rhs = jnp.where(j < s, gw_ref[...], wo_turned)
        tile = mm(wo_all[j // 2, j % 2], rhs).astype(bf16)
        tp[:, :, :, j * adapt : (j + 1) * adapt] = tile.reshape(SIDE, SIDE, shards, adapt)

    mid = layers * adapt // 2
    first = {}
    for off in (2, 1, 3):
        for n, axis in enumerate(("x", "z")):
            first[n, off] = new()
            to = step(axis, off)
            cut = pl.ds(n * mid, mid)
            src = tp.at[:, to, :, cut] if n == 0 else tp.at[to, :, :, cut]
            send(src, r1.at[n, off - 1], first[n, off], peer(axis, off))
    for off in range(1, shards):
        arrived(rr.at[shard_at(-off)], row_ids[off])
    tokens = mm(sel_ref[...], rr[...].reshape(shards * rr.shape[1], rr.shape[2]))
    own = tokens.shape[0] // layers
    for k in range(layers):
        sb[k, :own] = tokens[k * own : (k + 1) * own]
        sb[k, own : 2 * own, :] = jnp.zeros((own, sb.shape[2]), f32)
        for h in range(heads):
            line = sums[heads_by[h] : heads_by[h] + 3, adapt : 2 * adapt]
            sb[k, own + h : own + h + 1, :adapt] = jnp.sum(line, axis=0, keepdims=True)
    token_ids = [new() for _ in range(layers)]
    for off in range(1, layers):
        to = layer_at(off)
        send(sb.at[to], rq.at[s], token_ids[off], {"section": to, "dp": d})
    rq[s] = sb[s]
    second = {}
    for n in (0, 1):
        kept = tp[:, x, :, :mid] if n == 0 else tp[z, :, :, mid:]
        kept = kept.astype(f32)
        for off in (1, 3, 2):
            arrived(r1.at[n, off - 1], first[n, off])
            kept = kept + r1[n, off - 1].astype(f32)
        s1[n] = kept.astype(bf16)
        axis = ("z", "x")[n]
        for off in (2, 1, 3):
            second[n, off] = new()
            send(s1.at[n, step(axis, off)], r2.at[n, off - 1], second[n, off], peer(axis, off))
    gw_ring.relay()
    for n in (0, 1):
        kept = s1[n, me[("z", "x")[n]]].astype(f32)
        for off in (1, 3, 2):
            arrived(r2.at[n, off - 1], second[n, off])
            kept = kept + r2[n, off - 1].astype(f32)
        held[y, c, z, x, :, n * mid : (n + 1) * mid] = kept.astype(bf16)
    gather(lambda w, core, cut: held.at[w["y"], core, w["z"], w["x"], :, cut], layers * adapt)
    for off in range(1, layers):
        arrived(rq.at[layer_at(-off)], token_ids[off])
    for off in range(1, shards):
        src = x_all.at[c, shard_at(-off)]
        arrived(src, x_ids[off])
        send(src, src, x_swaps[off], twin)

    def tile(l, j):
        return held[l // 2, l % 2, :, :, :, j * adapt : (j + 1) * adapt].reshape(adapt, adapt)

    recurrence(layers, width, grad_scale, heads, tile, rq, side_ref, mine)
    swap = new()
    send(mine.at[1 - c], other, swap, twin)
    arrived(other, swap)
    a, b = mine[c], other[...]
    block[...] = jnp.concatenate([jnp.where(c == 0, a, b), jnp.where(c == 0, b, a)], axis=0).astype(
        bf16
    )
    pay[c, y, z, x] = block[...]

    def select():
        for off in range(1, shards):
            arrived(x_all.at[1 - c, shard_at(-off)], x_swaps[off])
        for copy in keep:
            copy.wait()
        quarter = x_sel.shape[0] // 4

        def batch(m, carried):
            start = pl.multiple_of(m * quarter, quarter)
            ids = lax.broadcasted_iota(jnp.int32, (quarter, place_ref.shape[1]), 0) + start
            seat = (ids == place_ref[...]).astype(f32).astype(bf16)
            for h in (0, 1):
                x_sel[pl.ds(start, quarter), h * wide : (h + 1) * wide] = mm(
                    seat, x_all[h].reshape(shards * rows, wide)
                ).astype(bf16)
            return carried

        lax.fori_loop(0, 4, batch, 0)

    gather(
        lambda w, core, cut: pay.at[core, w["y"], w["z"], w["x"], :, cut], block.shape[1], select
    )
    gw_ring.finish()
    gw_ring.twins()

    total = 2 * pay.shape[1] * shards * own

    def values(kind, at):
        cut = pl.ds(pl.multiple_of(at * adapt, adapt), adapt)
        return pay[kind, :, :, :, :, cut].reshape(total, adapt)

    def lanes(kind):
        return pay[kind, :, :, :, :, layers * adapt :].reshape(total, 128)

    act_t = values(0, s).T
    delta_t = values(1, s).T
    scal = lanes(0).astype(f32) + lanes(1).astype(f32)
    lane = lax.broadcasted_iota(jnp.int32, (total, 128), 1)
    sigma = jnp.sum(jnp.where(lane == s, scal, 0.0), axis=1, keepdims=True)
    head_sums = mm(act_t, lanes(0)) + mm(act_t, lanes(1))
    grad_out = -mm(act_t, (x_sel[...].astype(f32) * sigma).astype(bf16))
    for h in range(heads):
        grad_out += head_sums[:, layers + h : layers + h + 1] * head_ref[h : h + 1, :]
    grad_out_ref[...] = grad_out
    turned = sums_t
    turned[...] = mm(delta_t, x_sel[...])

    def layer(j, carried):
        jy, jc = j // 2, j % 2
        by = jnp.sum(jnp.where(lane == jnp.maximum(j, s), scal, 0.0), axis=1, keepdims=True)
        acts = values(0, j)
        scaled = (acts.astype(f32) * -by).astype(bf16)
        grad_out_ref[...] += mm(mm(act_t, scaled).astype(bf16), wo_all[jy, jc])

        @pl.when(j > s)
        def _():
            grad_out_ref[...] += mm(mm(act_t, values(1, j)).astype(bf16), gw_all[jy, jc], NT)

        @pl.when(j < s)
        def _():
            turned[...] += mm(mm(delta_t, acts).astype(bf16), wo_all[jy, jc])

        return carried

    lax.fori_loop(0, layers, layer, 0)
    grad_in_ref[...] = (turned[...] * scale_ref[...]).T
    loss = jnp.sum(jnp.where(lane == layers + heads, scal, 0.0), axis=0, keepdims=True)
    loss_ref[...] = jnp.broadcast_to(jnp.sum(loss, axis=1, keepdims=True) / total, loss_ref.shape)
    for copy in issued:
        copy.wait_send()


def recurrence(layers, width, grad_scale, heads, tile, rows_ref, side_ref, out_ref):
    adapt = 256
    own = side_ref.shape[0]
    sums = rows_ref[0, :own, 2 * adapt :]
    side = side_ref[...]
    part = lambda k: sums[:, k : k + 1] + sums[:, 1 + heads + k : 2 + heads + k]
    sq = part(0)
    est = [part(1 + k) for k in range(heads)]
    mask = side[:, 0:1]
    target = [side[:, 1 + k : 2 + k] for k in range(heads)]
    coef = [side[:, 4 + k : 5 + k] for k in range(heads)]
    into = [rows_ref[k, :own, :adapt] for k in range(layers)]
    onto = [rows_ref[k, :own, adapt : 2 * adapt] for k in range(layers)]
    head_out = [
        [rows_ref[k, own + h : own + h + 1, :adapt] for h in range(heads)] for k in range(layers)
    ]
    pre, fac, kept = [], [], {}
    for j in range(layers):
        f = lax.rsqrt(jnp.maximum(sq, 0.0) / width + EPS)
        p = f * into[j]
        act = (p * jax.nn.sigmoid(p)).astype(bf16)
        wide = act.astype(f32)
        out_ref[0, :, j * adapt : (j + 1) * adapt] = wide
        pre.append(p)
        fac.append(f)
        for k in range(j):
            kept[j, k] = onto[k]
        before = onto[j]
        for k in range(layers):
            if k <= j:
                onto[k] = onto[k] + mm(act, tile(k, j))
            else:
                into[k] = into[k] + mm(act, tile(k, j))
                onto[k] = onto[k] + mm(act, tile(j, k), NT)
        sq = sq + jnp.sum(wide * (before + onto[j]), axis=1, keepdims=True)
        for h in range(heads):
            est[h] = est[h] + jnp.sum(wide * head_out[j][h], axis=1, keepdims=True)
    f = lax.rsqrt(jnp.maximum(sq, 0.0) / width + EPS)
    loss = jnp.zeros_like(sq)
    along = jnp.zeros_like(sq)
    lane = lax.broadcasted_iota(jnp.int32, (own, 128), 1)
    extra = jnp.zeros(lane.shape, f32)
    grads = []
    for h in range(heads):
        e = f * est[h]
        err = e - target[h]
        weighted = coef[h] * mask * err
        loss = loss + 0.5 * weighted * err
        scaled = weighted * grad_scale
        along = along + scaled * e
        grads.append(f * scaled)
        extra = jnp.where(lane == layers + h, grads[h], extra)
    extra = jnp.where(lane == layers + heads, loss, extra)
    total = f * f * along / width
    back = []
    for k in range(layers):
        start = -total * onto[k]
        for h in range(heads):
            start = start + grads[h] * head_out[k][h]
        back.append(start)
    for l in range(layers - 1, -1, -1):
        extra = jnp.where(lane == l, total, extra)
        sg = jax.nn.sigmoid(pre[l])
        delta = (fac[l] * (back[l] * sg * (1.0 + pre[l] * (1.0 - sg)))).astype(bf16)
        wide = delta.astype(f32)
        out_ref[1, :, l * adapt : (l + 1) * adapt] = wide
        s = fac[l] / width * jnp.sum(wide * pre[l], axis=1, keepdims=True)
        total = total + s
        for k in range(l):
            back[k] = back[k] + mm(delta, tile(l, k), NT) - s * kept[l, k]
    high = extra.astype(bf16).astype(f32)
    out_ref[0, :, layers * adapt :] = high
    out_ref[1, :, layers * adapt :] = extra - high


def local(
    hidden,
    lengths,
    response_mask,
    norm_gain,
    weight_in,
    weight_out,
    final_gain,
    value_heads,
    old_values,
    advantages,
    multipliers,
):
    shards = lax.axis_size("dp")
    layers = lax.axis_size("section")
    d = lax.axis_index("dp")
    l = lax.axis_index("section")
    micro, cap, width = hidden.shape
    heads = value_heads.shape[0]
    adapt = weight_in.shape[2]
    total = micro * BAL * shards
    part = width // shards
    own = total // (shards * layers)
    per_micro = total // micro

    gain = norm_gain[0]
    scale_sl = lax.dynamic_slice(gain, (d * part,), (part,))
    gw_sl = lax.dynamic_slice(weight_in[0], (d * part, 0), (part, adapt))
    gw_sl = (scale_sl[:, None] * gw_sl.astype(f32)).astype(bf16)

    gfh = final_gain * value_heads
    head_sl = lax.dynamic_slice(gfh, (0, d * part), (heads, part))
    head_sl = jnp.concatenate([head_sl, jnp.zeros((8 - heads, part), f32)], axis=0)
    terms = jnp.stack(split(gfh, 3), axis=1).reshape(3 * heads, width)
    x0 = jnp.concatenate(
        [
            hidden.reshape(micro * cap, width),
            terms,
            jnp.zeros((128 - 3 * heads, width), bf16),
        ],
        axis=0,
    )
    ends = jnp.cumsum(lengths, axis=1)
    begins = ends - lengths
    offsets = jnp.arange(cap, dtype=jnp.int32)
    batches = jnp.arange(micro, dtype=jnp.int32)
    most = 3
    begin = jnp.take(begins, d, axis=1)[:, None]
    p = begin + offsets[None]
    n = p // shards - (begin - p % shards + shards - 1) // shards
    slot = (p % shards) * 16 + batches[:, None] * most + n
    slot = jnp.where(offsets[None] < jnp.take(lengths, d, axis=1)[:, None], slot, -1).reshape(-1)
    put = (jnp.arange(shards * 16, dtype=jnp.int32)[:, None] == slot[None]).astype(bf16)
    q = (begins - d + shards - 1) // shards
    p = d + shards * (q[:, :, None] + jnp.arange(most, dtype=jnp.int32))
    seat = (2 * batches[:, None, None] + p // 128) * own + (p // shards) % own
    seat = jnp.where(p < ends[:, :, None], seat, -1)
    seat = jnp.swapaxes(seat, 0, 1).reshape(shards, micro * most)
    seat = jnp.pad(seat, ((0, 0), (0, 16 - micro * most)), constant_values=-1).reshape(-1)
    sel = (jnp.arange(layers * own, dtype=jnp.int32)[:, None] == seat[None]).astype(bf16)

    token = jnp.where(
        offsets[None, None, :] < lengths[:, :, None],
        begins[:, :, None] + offsets[None, None, :],
        -1,
    )
    batch = l // 2
    ids = (l % 2) * 128 + shards * jnp.arange(own, dtype=jnp.int32) + d
    spot = lax.dynamic_index_in_dim(token, batch, 0, keepdims=False).reshape(-1)
    pick = (ids[:, None] == spot[None, :]).astype(f32)
    used = lax.dynamic_index_in_dim(response_mask, batch, 0, keepdims=False).astype(f32)
    aims = lax.dynamic_index_in_dim(old_values + advantages, batch, 1, keepdims=False)
    mask = jnp.sum(pick * used[None, :], axis=1, keepdims=True)
    aim = jnp.sum(pick[:, None, :] * aims[None], axis=2)
    coef = jnp.concatenate([jnp.ones((1,), f32), multipliers])
    side = jnp.concatenate(
        [
            mask,
            aim,
            jnp.broadcast_to(coef[None], (own, heads)),
            jnp.zeros((own, 127 - 2 * heads), f32),
        ],
        axis=1,
    )

    place = (batches[:, None, None] * shards + token % shards) * 16 + token // 128 * own
    place = jnp.where(token >= 0, place + token // shards % own, -1)
    place = jnp.swapaxes(place, 0, 1).reshape(1, -1)

    vm = pl.BlockSpec(memory_space=pltpu.VMEM)
    hbm = pl.BlockSpec(memory_space=pl.ANY)
    columns = layers * adapt + 128
    wide = 2 * adapt + 128
    half = layers * adapt // 2
    grad_in, grad_out, loss = pl.pallas_call(
        functools.partial(kernel, layers, float(width), LOSS_SCALE / total),
        out_shape=(
            jax.ShapeDtypeStruct((part, adapt), f32),
            jax.ShapeDtypeStruct((adapt, part), f32),
            jax.ShapeDtypeStruct((8, 128), f32),
        ),
        in_specs=[hbm, hbm] + [vm] * 9,
        out_specs=(vm, vm, vm),
        scratch_shapes=[
            pltpu.VMEM((shards, part, adapt), bf16),
            pltpu.VMEM((shards, adapt, part), bf16),
            pltpu.VMEM((x0.shape[0], wide), f32),
            pltpu.VMEM((SIDE, 2, adapt, part), bf16),
            pltpu.VMEM((SIDE, 2, part, adapt), bf16),
            pltpu.VMEM((2, shards, micro * cap, part // 2), bf16),
            pltpu.VMEM((total, part), bf16),
            pltpu.VMEM((2, SIDE, SIDE, SIDE, 16, columns), bf16),
            pltpu.VMEM((shards, 16, wide), bf16),
            pltpu.VMEM((SIDE, SIDE, 16, layers * adapt), bf16),
            pltpu.VMEM((2, 3, SIDE, 16, half), bf16),
            pltpu.VMEM((2, SIDE, 16, half), bf16),
            pltpu.VMEM((2, 3, 16, half), bf16),
            pltpu.VMEM((SIDE, 2, SIDE, SIDE, 16, layers * adapt), bf16),
            pltpu.VMEM((shards, 16, wide), bf16),
            pltpu.VMEM((layers, 2 * own, wide), f32),
            pltpu.VMEM((layers, 2 * own, wide), f32),
            pltpu.VMEM((2, own, columns), f32),
            pltpu.VMEM((own, columns), f32),
            pltpu.VMEM((16, columns), bf16),
            pltpu.VMEM((adapt, part), f32),
            pltpu.SemaphoreType.DMA((COPIES,)),
            pltpu.SemaphoreType.DMA((COPIES,)),
            pltpu.SemaphoreType.DMA((40,)),
        ],
        compiler_params=pltpu.CompilerParams(
            vmem_limit_bytes=60 * 1024 * 1024, collective_id=0, has_side_effects=True
        ),
        cost_estimate=pl.CostEstimate(
            flops=10**10, bytes_accessed=3 * 10**7, transcendentals=0
        ),
        name="layers",
    )(
        weight_in[0],
        weight_out[0],
        gw_sl,
        gain[None],
        x0,
        put,
        sel,
        side,
        place,
        head_sl,
        scale_sl[None],
    )
    return (grad_in[None], grad_out[None], loss[0, 0])


def solution(mesh):
    return jax.shard_map(
        local,
        mesh=mesh,
        in_specs=(
            P(None, "dp", None),
            P(),
            P(),
            P("section", None),
            P("section", None, None),
            P("section", None, None),
            P(),
            P(),
            P(),
            P(),
            P(),
        ),
        out_specs=(P("section", "dp", None), P("section", None, "dp"), P()),
        check_vma=False,
    )
```

```python
import functools

import jax
import jax.numpy as jnp
from jax import lax
from jax.experimental import pallas as pl
from jax.experimental.pallas import tpu as pltpu
from jax.sharding import PartitionSpec as P

EPS = 1e-05
LOSS_SCALE = 4096.0
BAL = 16

f32 = jnp.float32
bf16 = jnp.bfloat16
NT = (((1,), (1,)), ((), ()))
TN = (((0,), (0,)), ((), ()))
NN = (((1,), (0,)), ((), ()))
MESH = pl.DeviceIdType.MESH
SIDE = 4
COPIES = 360


def mm(a, b, dims=NN):
    return lax.dot_general(a, b, dims, preferred_element_type=f32)


def kernel(
    layers,
    width,
    grad_scale,
    lengths_ref,
    coef_ref,
    win_ref,
    wout_ref,
    gain_ref,
    hid_ref,
    final_ref,
    head_ref,
    mask_ref,
    old_ref,
    adv_ref,
    grad_in_ref,
    grad_out_ref,
    loss_ref,
    win,
    wout,
    sums,
    est,
    xf,
    terms,
    tokens_at,
    xm,
    wo_all,
    gw_all,
    x_all,
    x_sel,
    pay,
    rb,
    tp,
    r1,
    s1,
    r2,
    held,
    rr,
    sb,
    rq,
    mine,
    other,
    block,
    sums_t,
    send_sem,
    recv_sem,
    local_sem,
):
    s = lax.axis_index("section")
    d = lax.axis_index("dp")
    y, c = s // 2, s % 2
    z, x = d // SIDE, d % SIDE
    me = {"x": x, "y": y, "z": z}
    shards = SIDE * SIDE
    chunks, part, adapt = win.shape
    heads = head_ref.shape[0]
    micro, cap = hid_ref.shape[:2]
    rows = micro * cap
    step = lambda a, off: (me[a] + off + SIDE) % SIDE

    def peer(axis, off):
        if axis == "x":
            return {"section": s, "dp": z * SIDE + step("x", off)}
        if axis == "z":
            return {"section": s, "dp": step("z", off) * SIDE + x}
        return {"section": step("y", off) * 2 + c, "dp": d}

    twin = {"section": y * 2 + (1 - c), "dp": d}

    def shard_at(off):
        return (d + off + shards) % shards

    def layer_at(off):
        return (s + off + layers) % layers

    barrier = pltpu.get_barrier_semaphore()
    for off in range(1, shards):
        pl.semaphore_signal(
            barrier, inc=1, device_id={"section": s, "dp": shard_at(off)}, device_id_type=MESH
        )
    for off in range(1, layers):
        pl.semaphore_signal(
            barrier, inc=1, device_id={"section": layer_at(off), "dp": d}, device_id_type=MESH
        )
    pl.semaphore_wait(barrier, shards + layers - 2)

    issued = []
    count = [0, 0]

    def new():
        count[0] += 1
        return count[0] - 1

    def remote(src, dst, at, to):
        return pltpu.make_async_remote_copy(
            src_ref=src,
            dst_ref=dst,
            send_sem=send_sem.at[at],
            recv_sem=recv_sem.at[at],
            device_id=to,
            device_id_type=MESH,
        )

    def send(src, dst, at, to):
        copy = remote(src, dst, at, to)
        copy.start()
        issued.append(copy)

    def arrived(dst, at):
        remote(dst, dst, at, twin).wait_recv()

    def local(src, dst):
        count[1] += 1
        copy = pltpu.make_async_copy(src, dst, local_sem.at[count[1] - 1])
        copy.start()
        return copy

    class Ring:
        def __init__(self, axis, slab, swaps=False):
            self.slab = slab
            self.ids = [new() for _ in range(6)]
            self.plus, self.minus = peer(axis, 1), peer(axis, -1)
            self.swaps = {}
            if swaps:
                for v in (0, -1, 1, 2):
                    for h in (0, 1):
                        self.swaps[v, h] = new()

        def send(self, v, h, n, to):
            ref = self.slab(v, h, c)
            send(ref, ref, self.ids[n], to)

        def wait(self, v, h, n):
            arrived(self.slab(v, h, c), self.ids[n])
            self.swap(v, h)

        def swap(self, v, h):
            if self.swaps:
                ref = self.slab(v, h, c)
                send(ref, ref, self.swaps[v, h], twin)

        def start(self):
            self.send(0, 0, 0, self.plus)
            self.send(0, 1, 2, self.minus)
            self.send(0, 1, 1, self.plus)
            self.send(0, 0, 3, self.minus)
            self.swap(0, 0)
            self.swap(0, 1)

        def relay(self):
            arrived(self.slab(-1, 0, c), self.ids[0])
            self.send(-1, 0, 4, self.plus)
            arrived(self.slab(1, 1, c), self.ids[2])
            self.send(1, 1, 5, self.minus)
            self.swap(-1, 0)
            self.swap(1, 1)

        def finish(self):
            self.wait(-1, 1, 1)
            self.wait(1, 0, 3)
            self.wait(2, 0, 4)
            self.wait(2, 1, 5)

        def twins(self):
            for (v, h), at in self.swaps.items():
                arrived(self.slab(v, h, 1 - c), at)

    def gather(at, columns, meanwhile=None):
        third = (columns // 384) * 128
        bounds = [0, third, 2 * third, columns]
        orders = [("x", "z", "y"), ("z", "y", "x"), ("y", "x", "z")]
        parts = range(3)

        def ref(p, core, *steps):
            where = {
                axis: pl.ds(0, SIDE) if v is None else step(axis, v)
                for axis, v in zip(orders[p], steps)
            }
            return at(where, core, pl.ds(bounds[p], bounds[p + 1] - bounds[p]))

        ids, swaps = {}, {}

        def put(at_, block, to):
            ids[at_] = new()
            send(block, block, ids[at_], to)

        def swap(p, row, v):
            swaps[p, row, v] = new()
            block = ref(p, c, None, row, v)
            send(block, block, swaps[p, row, v], twin)

        def ring(p, row):
            axis = orders[p][2]
            for off in (1, -1):
                put((p, row, off), ref(p, c, None, row, 0), peer(axis, off))
            swap(p, row, 0)

        way = {0: 1, -1: -1, -3: 1, -2: -1}

        def relay(p, row):
            g = way[row]
            block = ref(p, c, None, row, -g)
            arrived(block, ids[p, row, g])
            put((p, row, 2), block, peer(orders[p][2], g))
            swap(p, row, -g)

        def end(p, row, v, n):
            arrived(ref(p, c, None, row, v), ids[p, row, n])
            swap(p, row, v)

        for off in (2, 1, 3):
            for p in parts:
                put((0, p, off, "a"), ref(p, c, 0, 0, 0), peer(orders[p][0], off))
        for off in (1, 3, 2):
            for p in parts:
                arrived(ref(p, c, -off, 0, 0), ids[0, p, off, "a"])
        for off in (2, 1, 3):
            for p in parts:
                put((1, p, off, "b"), ref(p, c, None, 0, 0), peer(orders[p][1], off))
        for p in parts:
            ring(p, 0)
        for off in (1, 3):
            for p in parts:
                arrived(ref(p, c, None, -off, 0), ids[1, p, off, "b"])
                ring(p, -off)
        for p in parts:
            relay(p, 0)
        for p in parts:
            arrived(ref(p, c, None, -2, 0), ids[1, p, 2, "b"])
            ring(p, -2)
        if meanwhile is not None:
            meanwhile()
        order = (0, -1, -3, -2)
        for row in order[1:]:
            for p in parts:
                relay(p, row)
        for row in order:
            for p in parts:
                end(p, row, way[row], -way[row])
        for row in order:
            for p in parts:
                end(p, row, 2, 2)
        for (p, row, v), at_ in swaps.items():
            arrived(ref(p, 1 - c, None, row, v), at_)

    chunks = win.shape[0]
    loads = []
    for k in range(chunks):
        loads.append(local(win_ref.at[pl.ds(k * part, part)], win.at[k]))
        loads.append(local(wout_ref.at[:, pl.ds(k * part, part)], wout.at[k]))

    half = adapt // 2
    wo_ring = Ring(
        "y", lambda v, h, core: wo_all.at[step("y", v), core, pl.ds(h * half, half)], True
    )
    columns = pl.ds(pl.multiple_of(d * part, part), part)
    local(wout_ref.at[:, columns], wo_all.at[y, c]).wait()
    wo_ring.start()
    wide = part // 2
    keep = []
    for h in (0, 1):
        keep.append(
            local(
                hid_ref.at[:, :, pl.ds(pl.multiple_of(d * part + h * wide, wide), wide)],
                x_all.at[h, d],
            )
        )
    x_ids = [new() for _ in range(shards)]
    x_swaps = [new() for _ in range(shards)]
    for off in range(1, shards):
        to = shard_at(off)
        send(
            hid_ref.at[:, :, pl.ds(pl.multiple_of(to * part + c * wide, wide), wide)],
            x_all.at[c, d],
            x_ids[off],
            {"section": s, "dp": to},
        )
    gw_ring = Ring(
        "y", lambda v, h, core: gw_all.at[step("y", v), core, pl.ds(h * half, half)], True
    )

    begin = [[None] * shards for _ in range(micro)]
    length = [[lengths_ref[m, i] for i in range(shards)] for m in range(micro)]
    mine_at = []
    for m in range(micro):
        at, here = jnp.int32(0), jnp.int32(0)
        for i in range(shards):
            begin[m][i] = at
            here = here + jnp.where(i < d, length[m][i], 0)
            at = at + length[m][i]
        mine_at.append(here)
    lane = lax.broadcasted_iota(jnp.int32, (1, rows), 1)
    m_of, b_of, n_of = jnp.zeros_like(lane), jnp.zeros_like(lane), jnp.zeros_like(lane)
    for m in range(micro):
        m_of = jnp.where(lane >= m * cap, m, m_of)
        b_of = jnp.where(lane >= m * cap, mine_at[m], b_of)
        n_of = jnp.where(lane >= m * cap, lengths_ref[m, d], n_of)
    r_of = lane - m_of * cap
    p = b_of + r_of
    n = (p >> 4) - ((b_of - (p & 15) + 15) >> 4)
    slot = jnp.where(r_of < n_of, (p & 15) * 16 + m_of * 3 + n, -1)
    put_rows = lax.broadcasted_iota(jnp.int32, (shards * 16, rows), 0) == slot
    put_rows = jnp.where(put_rows, 1.0, 0.0).astype(bf16)
    lane = lax.broadcasted_iota(jnp.int32, (1, shards * 16), 1)
    src, n = lane >> 4, lane & 15
    m_of = jnp.where(n >= 3, 1, 0) + jnp.where(n >= 6, 1, 0) + jnp.where(n >= 9, 1, 0)
    b_of, n_of = jnp.zeros_like(lane), jnp.zeros_like(lane)
    for m in range(micro):
        b, e = jnp.zeros_like(lane), jnp.zeros_like(lane)
        for i in range(shards):
            b = jnp.where(src == i, begin[m][i], b)
            e = jnp.where(src == i, begin[m][i] + length[m][i], e)
        b_of = jnp.where(m_of == m, b, b_of)
        n_of = jnp.where(m_of == m, e, n_of)
    p = d + 16 * (((b_of - d + 15) >> 4) + n - 3 * m_of)
    seat = (2 * m_of + (p >> 7)) * 8 + ((p >> 4) & 7)
    seat = jnp.where(p < n_of, jnp.where(n < 12, seat, -1), -1)
    take_rows = lax.broadcasted_iota(jnp.int32, (layers * 8, shards * 16), 0) == seat
    take_rows = jnp.where(take_rows, 1.0, 0.0).astype(bf16)
    lane = lax.broadcasted_iota(jnp.int32, (1, shards * cap), 1)
    ids = lax.broadcasted_iota(jnp.int32, (8, shards * cap), 0) * 16 + (s % 2) * 128 + d
    batch = s // 2
    spot = jnp.zeros_like(lane)
    used = jnp.zeros(lane.shape, f32)
    aims = [jnp.zeros(lane.shape, f32) for _ in range(heads)]
    for m in range(micro):
        b, e, first_lane = jnp.zeros_like(lane), jnp.zeros_like(lane), jnp.zeros_like(lane)
        for i in range(shards):
            b = jnp.where(lane >= i * cap, begin[m][i], b)
            e = jnp.where(lane >= i * cap, length[m][i], e)
            first_lane = jnp.where(lane >= i * cap, i * cap, first_lane)
        row = lane - first_lane
        row = jnp.where(row < e, b + row, -1)
        tokens_at[m] = row
        spot = jnp.where(batch == m, row, spot)
        used = jnp.where(batch == m, mask_ref[m : m + 1, :].astype(f32), used)
        for h in range(heads):
            aim = old_ref[h, m : m + 1, :] + adv_ref[h, m : m + 1, :]
            aims[h] = jnp.where(batch == m, aim, aims[h])
    pick = ids == spot
    mask = jnp.sum(jnp.where(pick, used, 0.0), axis=1, keepdims=True)
    target = [jnp.sum(jnp.where(pick, aim, 0.0), axis=1, keepdims=True) for aim in aims]

    square = jnp.zeros((rows, 128), f32)
    sums[...] = jnp.zeros(sums.shape, f32)
    est[...] = jnp.zeros(est.shape, f32)
    terms[...] = jnp.zeros(terms.shape, f32)
    for copy in loads:
        copy.wait()

    def chunk(k, square):
        cut = pl.ds(pl.multiple_of(k * part, part), part)
        for m in range(micro):
            xf[m * cap : (m + 1) * cap, :] = hid_ref[m, :, cut].astype(f32)
        left = final_ref[:, cut] * head_ref[:, cut]
        for t in range(3):
            term = left.astype(bf16).astype(f32)
            terms[8 * t : 8 * t + heads, :] = term
            left = left - term
        x = xf[...]
        for i in range(part // 128):
            piece = x[:, i * 128 : (i + 1) * 128]
            square = square + piece * piece
        lines = terms[...].astype(bf16)
        x16 = x.astype(bf16)
        both = jnp.concatenate([x16, lines], axis=0)
        sums[:rows, :adapt] += mm((x * gain_ref[:, cut]).astype(bf16), win[k])
        sums[:, adapt : 2 * adapt] += mm(both, wout[k], NT)
        est[...] += mm(x16, lines, NT)
        return square

    square = lax.fori_loop(0, chunks // 2, chunk, square)
    wo_ring.relay()
    square = lax.fori_loop(chunks // 2, chunks, chunk, square)
    square = jnp.sum(square, axis=1, keepdims=True)
    gw_own = (win[d].astype(f32).T * gain_ref[:, columns]).astype(bf16)
    gw_all[y, c] = gw_own
    lane = lax.broadcasted_iota(jnp.int32, (rows, 128), 1)
    dots = [square]
    for h in range(heads):
        dots.append(est[:, h : h + 1] + est[:, 8 + h : 9 + h] + est[:, 16 + h : 17 + h])
    own_side = jnp.zeros((rows, 128), f32)
    for k, v in enumerate(dots):
        high = v.astype(bf16).astype(f32)
        own_side = jnp.where(lane == k, high, own_side)
        own_side = jnp.where(lane == len(dots) + k, v - high, own_side)
    ab = jnp.concatenate([sums[:rows, :], own_side], axis=1).astype(bf16)
    rb[...] = mm(put_rows, ab).astype(bf16).reshape(rb.shape)

    row_ids = [new() for _ in range(shards)]
    for off in range(1, shards):
        to = shard_at(off)
        send(rb.at[to], rr.at[d], row_ids[off], {"section": s, "dp": to})
    rr[d] = rb[d]

    wo_ring.finish()
    wo_ring.twins()
    gw_ring.start()

    wo_own = wo_all[y, c]
    for j in range(layers):
        rhs = jnp.where(j < s, gw_own, wo_own)
        tile = mm(wo_all[j // 2, j % 2], rhs, NT).astype(bf16)
        tp[:, :, :, j * adapt : (j + 1) * adapt] = tile.reshape(SIDE, SIDE, shards, adapt)

    mid = layers * adapt // 2
    first = {}
    for off in (2, 1, 3):
        for n, axis in enumerate(("x", "z")):
            first[n, off] = new()
            to = step(axis, off)
            cut = pl.ds(n * mid, mid)
            src = tp.at[:, to, :, cut] if n == 0 else tp.at[to, :, :, cut]
            send(src, r1.at[n, off - 1], first[n, off], peer(axis, off))
    for off in range(1, shards):
        arrived(rr.at[shard_at(-off)], row_ids[off])
    tokens = mm(take_rows, rr[...].reshape(shards * rr.shape[1], rr.shape[2]))
    own = tokens.shape[0] // layers
    lines = []
    for h in range(heads):
        at = rows + h
        lines.append(sum(sums[at + 8 * t : at + 8 * t + 1, adapt:] for t in range(3)))
    for k in range(layers):
        sb[k, :own] = tokens[k * own : (k + 1) * own]
        sb[k, own : 2 * own, :] = jnp.zeros((own, sb.shape[2]), f32)
        for h in range(heads):
            sb[k, own + h : own + h + 1, :adapt] = lines[h]
    token_ids = [new() for _ in range(layers)]
    for off in range(1, layers):
        to = layer_at(off)
        send(sb.at[to], rq.at[s], token_ids[off], {"section": to, "dp": d})
    rq[s] = sb[s]
    second = {}
    for n in (0, 1):
        kept = tp[:, x, :, :mid] if n == 0 else tp[z, :, :, mid:]
        kept = kept.astype(f32)
        for off in (1, 3, 2):
            arrived(r1.at[n, off - 1], first[n, off])
            kept = kept + r1[n, off - 1].astype(f32)
        s1[n] = kept.astype(bf16)
        axis = ("z", "x")[n]
        for off in (2, 1, 3):
            second[n, off] = new()
            send(s1.at[n, step(axis, off)], r2.at[n, off - 1], second[n, off], peer(axis, off))
    gw_ring.relay()
    for off in range(1, shards):
        src = x_all.at[c, shard_at(-off)]
        arrived(src, x_ids[off])
        send(src, src, x_swaps[off], twin)
    for n in (0, 1):
        kept = s1[n, me[("z", "x")[n]]].astype(f32)
        for off in (1, 3, 2):
            arrived(r2.at[n, off - 1], second[n, off])
            kept = kept + r2[n, off - 1].astype(f32)
        held[y, c, z, x, :, n * mid : (n + 1) * mid] = kept.astype(bf16)
    gather(lambda w, core, cut: held.at[w["y"], core, w["z"], w["x"], :, cut], layers * adapt)
    for off in range(1, layers):
        arrived(rq.at[layer_at(-off)], token_ids[off])

    def tile(l, j):
        return held[l // 2, l % 2, :, :, :, j * adapt : (j + 1) * adapt].reshape(adapt, adapt)

    coef = [1.0, coef_ref[0], coef_ref[1]]
    recurrence(layers, width, grad_scale, tile, rq, mask, target, coef, mine)
    swap = new()
    send(mine.at[1 - c], other, swap, twin)
    arrived(other, swap)
    a, b = mine[c], other[...]
    block[...] = jnp.concatenate([jnp.where(c == 0, a, b), jnp.where(c == 0, b, a)], axis=0).astype(
        bf16
    )
    pay[c, y, z, x] = block[...]

    def select():
        for off in range(1, shards):
            arrived(x_all.at[1 - c, shard_at(-off)], x_swaps[off])
        for copy in keep:
            copy.wait()
        quarter = x_sel.shape[1] // micro
        at = lax.broadcasted_iota(jnp.int32, (quarter, shards * cap), 0)
        token = ((at >> 3) & 1) * 128 + (at & 7) * 16 + (at >> 4)

        def batch(i, carried):
            m, h = i // 2, i % 2
            for src in range(shards):
                xm[src * cap : (src + 1) * cap, :] = x_all[h, src, m].astype(f32)
            seat = jnp.where(token == tokens_at[m], 1.0, 0.0).astype(bf16)
            start = pl.multiple_of(m * quarter, quarter)
            x_sel[h, pl.ds(start, quarter), :] = mm(seat, xm[...].astype(bf16)).astype(bf16)
            return carried

        lax.fori_loop(0, 2 * micro, batch, 0)

    gather(
        lambda w, core, cut: pay.at[core, w["y"], w["z"], w["x"], :, cut], block.shape[1], select
    )
    gw_ring.finish()
    gw_ring.twins()

    total = 2 * pay.shape[1] * shards * own

    def values(kind, at):
        cut = pl.ds(pl.multiple_of(at * adapt, adapt), adapt)
        return pay[kind, :, :, :, :, cut].reshape(total, adapt)

    def lanes(kind):
        return pay[kind, :, :, :, :, layers * adapt :].reshape(total, 128)

    act_t = values(0, s).T
    delta_t = values(1, s).T
    scal = lanes(0).astype(f32) + lanes(1).astype(f32)
    lane = lax.broadcasted_iota(jnp.int32, (total, 128), 1)
    sigma = jnp.sum(jnp.where(lane == s, scal, 0.0), axis=1, keepdims=True)
    head_sums = mm(act_t, lanes(0)) + mm(act_t, lanes(1))
    turned = sums_t
    for n in (0, 1):
        cut = slice(n * wide, (n + 1) * wide)
        grad_out_ref[:, cut] = -mm(act_t, (x_sel[n].astype(f32) * sigma).astype(bf16))
        turned[:, cut] = mm(delta_t, x_sel[n])
    gfh = final_ref[:, columns] * head_ref[:, columns]
    for h in range(heads):
        grad_out_ref[...] += head_sums[:, layers + h : layers + h + 1] * gfh[h : h + 1, :]

    def layer(j, carried):
        jy, jc = j // 2, j % 2
        by = jnp.sum(jnp.where(lane == jnp.maximum(j, s), scal, 0.0), axis=1, keepdims=True)
        acts = values(0, j)
        scaled = (acts.astype(f32) * -by).astype(bf16)
        grad_out_ref[...] += mm(mm(act_t, scaled).astype(bf16), wo_all[jy, jc])

        @pl.when(j > s)
        def _():
            grad_out_ref[...] += mm(mm(act_t, values(1, j)).astype(bf16), gw_all[jy, jc])

        @pl.when(j < s)
        def _():
            turned[...] += mm(mm(delta_t, acts).astype(bf16), wo_all[jy, jc])

        return carried

    lax.fori_loop(0, layers, layer, 0)
    grad_in_ref[...] = (turned[...] * gain_ref[:, columns]).T
    loss = jnp.sum(jnp.where(lane == layers + heads, scal, 0.0), axis=0, keepdims=True)
    loss_ref[0, 0] = jnp.sum(loss) / total
    for copy in issued:
        copy.wait_send()


def recurrence(layers, width, grad_scale, tile, rows_ref, mask, target, coef, out_ref):
    adapt = 256
    heads = len(target)
    own = mask.shape[0]
    sums = rows_ref[0, :own, 2 * adapt :]
    part = lambda k: sums[:, k : k + 1] + sums[:, 1 + heads + k : 2 + heads + k]
    sq = part(0)
    est = [part(1 + k) for k in range(heads)]
    into = [rows_ref[k, :own, :adapt] for k in range(layers)]
    onto = [rows_ref[k, :own, adapt : 2 * adapt] for k in range(layers)]
    head_out = [
        [rows_ref[k, own + h : own + h + 1, :adapt] for h in range(heads)] for k in range(layers)
    ]
    pre, fac, kept = [], [], {}
    for j in range(layers):
        f = lax.rsqrt(jnp.maximum(sq, 0.0) / width + EPS)
        p = f * into[j]
        act = (p * jax.nn.sigmoid(p)).astype(bf16)
        wide = act.astype(f32)
        out_ref[0, :, j * adapt : (j + 1) * adapt] = wide
        pre.append(p)
        fac.append(f)
        for k in range(j):
            kept[j, k] = onto[k]
        before = onto[j]
        for k in range(layers):
            if k <= j:
                onto[k] = onto[k] + mm(act, tile(k, j))
            else:
                into[k] = into[k] + mm(act, tile(k, j))
                onto[k] = onto[k] + mm(act, tile(j, k), NT)
        sq = sq + jnp.sum(wide * (before + onto[j]), axis=1, keepdims=True)
        for h in range(heads):
            est[h] = est[h] + jnp.sum(wide * head_out[j][h], axis=1, keepdims=True)
    f = lax.rsqrt(jnp.maximum(sq, 0.0) / width + EPS)
    loss = jnp.zeros_like(sq)
    along = jnp.zeros_like(sq)
    lane = lax.broadcasted_iota(jnp.int32, (own, 128), 1)
    extra = jnp.zeros(lane.shape, f32)
    grads = []
    for h in range(heads):
        e = f * est[h]
        err = e - target[h]
        weighted = coef[h] * mask * err
        loss = loss + 0.5 * weighted * err
        scaled = weighted * grad_scale
        along = along + scaled * e
        grads.append(f * scaled)
        extra = jnp.where(lane == layers + h, grads[h], extra)
    extra = jnp.where(lane == layers + heads, loss, extra)
    total = f * f * along / width
    back = []
    for k in range(layers):
        start = -total * onto[k]
        for h in range(heads):
            start = start + grads[h] * head_out[k][h]
        back.append(start)
    for l in range(layers - 1, -1, -1):
        extra = jnp.where(lane == l, total, extra)
        sg = jax.nn.sigmoid(pre[l])
        delta = (fac[l] * (back[l] * sg * (1.0 + pre[l] * (1.0 - sg)))).astype(bf16)
        wide = delta.astype(f32)
        out_ref[1, :, l * adapt : (l + 1) * adapt] = wide
        s = fac[l] / width * jnp.sum(wide * pre[l], axis=1, keepdims=True)
        total = total + s
        for k in range(l):
            back[k] = back[k] + mm(delta, tile(l, k), NT) - s * kept[l, k]
    high = extra.astype(bf16).astype(f32)
    out_ref[0, :, layers * adapt :] = high
    out_ref[1, :, layers * adapt :] = extra - high


def local(
    hidden,
    lengths,
    response_mask,
    norm_gain,
    weight_in,
    weight_out,
    final_gain,
    value_heads,
    old_values,
    advantages,
    multipliers,
):
    shards = lax.axis_size("dp")
    layers = lax.axis_size("section")
    micro, cap, width = hidden.shape
    heads = value_heads.shape[0]
    adapt = weight_in.shape[2]
    total = micro * BAL * shards
    part = width // shards
    own = total // (shards * layers)

    sm = pl.BlockSpec(memory_space=pltpu.SMEM)
    vm = pl.BlockSpec(memory_space=pltpu.VMEM)
    hbm = pl.BlockSpec(memory_space=pl.ANY)
    columns = layers * adapt + 128
    wide = 2 * adapt + 128
    half = layers * adapt // 2
    grad_in, grad_out, loss = pl.pallas_call(
        functools.partial(kernel, layers, float(width), LOSS_SCALE / total),
        out_shape=(
            jax.ShapeDtypeStruct((part, adapt), f32),
            jax.ShapeDtypeStruct((adapt, part), f32),
            jax.ShapeDtypeStruct((1, 1), f32),
        ),
        in_specs=[sm, sm, hbm, hbm] + [vm] * 7,
        out_specs=(vm, vm, sm),
        scratch_shapes=[
            pltpu.VMEM((shards, part, adapt), bf16),
            pltpu.VMEM((shards, adapt, part), bf16),
            pltpu.VMEM((micro * cap + 32, 2 * adapt), f32),
            pltpu.VMEM((micro * cap, 32), f32),
            pltpu.VMEM((micro * cap, part), f32),
            pltpu.VMEM((32, part), f32),
            pltpu.VMEM((micro, 1, shards * cap), jnp.int32),
            pltpu.VMEM((shards * cap, part // 2), f32),
            pltpu.VMEM((SIDE, 2, adapt, part), bf16),
            pltpu.VMEM((SIDE, 2, adapt, part), bf16),
            pltpu.VMEM((2, shards, micro, cap, part // 2), bf16),
            pltpu.VMEM((2, total, part // 2), bf16),
            pltpu.VMEM((2, SIDE, SIDE, SIDE, 16, columns), bf16),
            pltpu.VMEM((shards, 16, wide), bf16),
            pltpu.VMEM((SIDE, SIDE, 16, layers * adapt), bf16),
            pltpu.VMEM((2, 3, SIDE, 16, half), bf16),
            pltpu.VMEM((2, SIDE, 16, half), bf16),
            pltpu.VMEM((2, 3, 16, half), bf16),
            pltpu.VMEM((SIDE, 2, SIDE, SIDE, 16, layers * adapt), bf16),
            pltpu.VMEM((shards, 16, wide), bf16),
            pltpu.VMEM((layers, 2 * own, wide), f32),
            pltpu.VMEM((layers, 2 * own, wide), f32),
            pltpu.VMEM((2, own, columns), f32),
            pltpu.VMEM((own, columns), f32),
            pltpu.VMEM((16, columns), bf16),
            pltpu.VMEM((adapt, part), f32),
            pltpu.SemaphoreType.DMA((COPIES,)),
            pltpu.SemaphoreType.DMA((COPIES,)),
            pltpu.SemaphoreType.DMA((40,)),
        ],
        compiler_params=pltpu.CompilerParams(
            vmem_limit_bytes=60 * 1024 * 1024, collective_id=0, has_side_effects=True
        ),
        cost_estimate=pl.CostEstimate(
            flops=10**10, bytes_accessed=3 * 10**7, transcendentals=0
        ),
        name="layers",
    )(
        lengths,
        multipliers,
        weight_in[0],
        weight_out[0],
        norm_gain,
        hidden,
        final_gain[None],
        value_heads,
        response_mask,
        old_values,
        advantages,
    )
    return (grad_in[None], grad_out[None], loss[0, 0])


def solution(mesh):
    return jax.shard_map(
        local,
        mesh=mesh,
        in_specs=(
            P(None, "dp", None),
            P(),
            P(),
            P("section", None),
            P("section", None, None),
            P("section", None, None),
            P(),
            P(),
            P(),
            P(),
            P(),
        ),
        out_specs=(P("section", "dp", None), P("section", None, "dp"), P()),
        check_vma=False,
    )
```

```python
import functools

import jax
import jax.numpy as jnp
from jax import lax
from jax.experimental import pallas as pl
from jax.experimental.pallas import tpu as pltpu
from jax.sharding import PartitionSpec as P

EPS = 1e-05
LOSS_SCALE = 4096.0
BAL = 16

f32 = jnp.float32
bf16 = jnp.bfloat16
NT = (((1,), (1,)), ((), ()))
TN = (((0,), (0,)), ((), ()))
NN = (((1,), (0,)), ((), ()))
MESH = pl.DeviceIdType.MESH
SIDE = 4
COPIES = 360


def mm(a, b, dims=NN):
    return lax.dot_general(a, b, dims, preferred_element_type=f32)


def kernel(
    layers,
    width,
    grad_scale,
    lengths_ref,
    coef_ref,
    win_ref,
    wout_ref,
    gain_ref,
    hid_ref,
    final_ref,
    head_ref,
    mask_ref,
    old_ref,
    adv_ref,
    grad_in_ref,
    grad_out_ref,
    loss_ref,
    win,
    wout,
    sums,
    est,
    terms,
    tokens_at,
    xm,
    weights,
    x_all,
    x_sel,
    pay,
    rb,
    tp,
    r1,
    s1,
    r2,
    held,
    rr,
    sb,
    rq,
    mine,
    other,
    block,
    acc,
    both_t,
    scal_t,
    send_sem,
    recv_sem,
    local_sem,
):
    s = lax.axis_index("section")
    d = lax.axis_index("dp")
    y, c = s // 2, s % 2
    z, x = d // SIDE, d % SIDE
    me = {"x": x, "y": y, "z": z}
    shards = SIDE * SIDE
    chunks, part, adapt = win.shape
    heads = head_ref.shape[0]
    cap, micro = hid_ref.shape[:2]
    rows = micro * cap
    step = lambda a, off: (me[a] + off + SIDE) % SIDE

    def peer(axis, off):
        if axis == "x":
            return {"section": s, "dp": z * SIDE + step("x", off)}
        if axis == "z":
            return {"section": s, "dp": step("z", off) * SIDE + x}
        return {"section": step("y", off) * 2 + c, "dp": d}

    twin = {"section": y * 2 + (1 - c), "dp": d}

    def shard_at(off):
        return (d + off + shards) % shards

    def layer_at(off):
        return (s + off + layers) % layers

    barrier = pltpu.get_barrier_semaphore()
    for off in range(1, shards):
        pl.semaphore_signal(
            barrier, inc=1, device_id={"section": s, "dp": shard_at(off)}, device_id_type=MESH
        )
    for off in range(1, layers):
        pl.semaphore_signal(
            barrier, inc=1, device_id={"section": layer_at(off), "dp": d}, device_id_type=MESH
        )
    pl.semaphore_wait(barrier, shards + layers - 2)

    issued = []
    count = [0, 0]

    def new():
        count[0] += 1
        return count[0] - 1

    def remote(src, dst, at, to):
        return pltpu.make_async_remote_copy(
            src_ref=src,
            dst_ref=dst,
            send_sem=send_sem.at[at],
            recv_sem=recv_sem.at[at],
            device_id=to,
            device_id_type=MESH,
        )

    def send(src, dst, at, to):
        copy = remote(src, dst, at, to)
        copy.start()
        issued.append(copy)

    def arrived(dst, at):
        remote(dst, dst, at, twin).wait_recv()

    def local(src, dst):
        count[1] += 1
        copy = pltpu.make_async_copy(src, dst, local_sem.at[count[1] - 1])
        copy.start()
        return copy

    class Ring:
        def __init__(self, axis, slab, swaps=False):
            self.slab = slab
            self.ids = [new() for _ in range(6)]
            self.plus, self.minus = peer(axis, 1), peer(axis, -1)
            self.swaps = {}
            if swaps:
                for v in (0, -1, 1, 2):
                    for h in (0, 1):
                        self.swaps[v, h] = new()

        def send(self, v, h, n, to):
            ref = self.slab(v, h, c)
            send(ref, ref, self.ids[n], to)

        def wait(self, v, h, n):
            arrived(self.slab(v, h, c), self.ids[n])
            self.swap(v, h)

        def swap(self, v, h):
            if self.swaps:
                ref = self.slab(v, h, c)
                send(ref, ref, self.swaps[v, h], twin)

        def start(self):
            self.send(0, 0, 0, self.plus)
            self.send(0, 1, 2, self.minus)
            self.send(0, 1, 1, self.plus)
            self.send(0, 0, 3, self.minus)
            self.swap(0, 0)
            self.swap(0, 1)

        def relay(self):
            arrived(self.slab(-1, 0, c), self.ids[0])
            self.send(-1, 0, 4, self.plus)
            arrived(self.slab(1, 1, c), self.ids[2])
            self.send(1, 1, 5, self.minus)
            self.swap(-1, 0)
            self.swap(1, 1)

        def finish(self):
            self.wait(-1, 1, 1)
            self.wait(1, 0, 3)
            self.wait(2, 0, 4)
            self.wait(2, 1, 5)

        def twins(self):
            for (v, h), at in self.swaps.items():
                arrived(self.slab(v, h, 1 - c), at)

    def gather(at, columns, meanwhile=None):
        third = (columns // 384) * 128
        bounds = [0, third, 2 * third, columns]
        orders = [("x", "z", "y"), ("z", "y", "x"), ("y", "x", "z")]
        parts = range(3)

        def ref(p, core, *steps):
            where = {
                axis: pl.ds(0, SIDE) if v is None else step(axis, v)
                for axis, v in zip(orders[p], steps)
            }
            return at(where, core, pl.ds(bounds[p], bounds[p + 1] - bounds[p]))

        ids, swaps = {}, {}

        def put(at_, block, to):
            ids[at_] = new()
            send(block, block, ids[at_], to)

        def swap(p, row, v):
            swaps[p, row, v] = new()
            block = ref(p, c, None, row, v)
            send(block, block, swaps[p, row, v], twin)

        def ring(p, row):
            axis = orders[p][2]
            for off in (1, -1):
                put((p, row, off), ref(p, c, None, row, 0), peer(axis, off))
            swap(p, row, 0)

        way = {0: 1, -1: -1, -3: 1, -2: -1}

        def relay(p, row):
            g = way[row]
            block = ref(p, c, None, row, -g)
            arrived(block, ids[p, row, g])
            put((p, row, 2), block, peer(orders[p][2], g))
            swap(p, row, -g)

        def end(p, row, v, n):
            arrived(ref(p, c, None, row, v), ids[p, row, n])
            swap(p, row, v)

        for off in (2, 1, 3):
            for p in parts:
                put((0, p, off, "a"), ref(p, c, 0, 0, 0), peer(orders[p][0], off))
        for off in (1, 3, 2):
            for p in parts:
                arrived(ref(p, c, -off, 0, 0), ids[0, p, off, "a"])
        for off in (2, 1, 3):
            for p in parts:
                put((1, p, off, "b"), ref(p, c, None, 0, 0), peer(orders[p][1], off))
        for p in parts:
            ring(p, 0)
        for off in (1, 3):
            for p in parts:
                arrived(ref(p, c, None, -off, 0), ids[1, p, off, "b"])
                ring(p, -off)
        for p in parts:
            relay(p, 0)
        for p in parts:
            arrived(ref(p, c, None, -2, 0), ids[1, p, 2, "b"])
            ring(p, -2)
        if meanwhile is not None:
            meanwhile()
        order = (0, -1, -3, -2)
        for row in order[1:]:
            for p in parts:
                relay(p, row)
        for row in order:
            for p in parts:
                end(p, row, way[row], -way[row])
        for row in order:
            for p in parts:
                end(p, row, 2, 2)
        for (p, row, v), at_ in swaps.items():
            arrived(ref(p, 1 - c, None, row, v), at_)

    wo_all, gw_all = weights.at[0], weights.at[1]

    chunks = win.shape[0]
    loads = []
    for k in range(chunks):
        loads.append(local(win_ref.at[pl.ds(k * part, part)], win.at[k]))
        loads.append(local(wout_ref.at[:, pl.ds(k * part, part)], wout.at[k]))

    half = adapt // 2
    wo_ring = Ring(
        "y", lambda v, h, core: wo_all.at[step("y", v), core, pl.ds(h * half, half)], True
    )
    columns = pl.ds(pl.multiple_of(d * part, part), part)
    local(wout_ref.at[:, columns], wo_all.at[y, c]).wait()
    wo_ring.start()
    wide = part // 2
    keep = []
    for h in (0, 1):
        keep.append(
            local(
                hid_ref.at[:, :, pl.ds(pl.multiple_of(d * part + h * wide, wide), wide)],
                x_all.at[h, d],
            )
        )
    x_ids = [new() for _ in range(shards)]
    x_swaps = [new() for _ in range(shards)]
    for off in range(1, shards):
        to = shard_at(off)
        send(
            hid_ref.at[:, :, pl.ds(pl.multiple_of(to * part + c * wide, wide), wide)],
            x_all.at[c, d],
            x_ids[off],
            {"section": s, "dp": to},
        )
    gw_ring = Ring(
        "y", lambda v, h, core: gw_all.at[step("y", v), core, pl.ds(h * half, half)], True
    )

    begin = [[None] * shards for _ in range(micro)]
    length = [[lengths_ref[m, i] for i in range(shards)] for m in range(micro)]
    mine_at = []
    for m in range(micro):
        at, here = jnp.int32(0), jnp.int32(0)
        for i in range(shards):
            begin[m][i] = at
            here = here + jnp.where(i < d, length[m][i], 0)
            at = at + length[m][i]
        mine_at.append(here)
    lane = lax.broadcasted_iota(jnp.int32, (1, rows), 1)
    b_of, n_of = jnp.zeros_like(lane), jnp.zeros_like(lane)
    m_of, r_of = lane & 3, lane >> 2
    for m in range(micro):
        b_of = jnp.where(m_of == m, mine_at[m], b_of)
        n_of = jnp.where(m_of == m, lengths_ref[m, d], n_of)
    p = b_of + r_of
    n = (p >> 4) - ((b_of - (p & 15) + 15) >> 4)
    slot = jnp.where(r_of < n_of, (p & 15) * 16 + m_of * 3 + n, -1)
    put_rows = lax.broadcasted_iota(jnp.int32, (shards * 16, rows), 0) == slot
    put_rows = jnp.where(put_rows, 1.0, 0.0).astype(bf16)
    lane = lax.broadcasted_iota(jnp.int32, (1, shards * 16), 1)
    src, n = lane >> 4, lane & 15
    m_of = jnp.where(n >= 3, 1, 0) + jnp.where(n >= 6, 1, 0) + jnp.where(n >= 9, 1, 0)
    b_of, n_of = jnp.zeros_like(lane), jnp.zeros_like(lane)
    for m in range(micro):
        b, e = jnp.zeros_like(lane), jnp.zeros_like(lane)
        for i in range(shards):
            b = jnp.where(src == i, begin[m][i], b)
            e = jnp.where(src == i, begin[m][i] + length[m][i], e)
        b_of = jnp.where(m_of == m, b, b_of)
        n_of = jnp.where(m_of == m, e, n_of)
    p = d + 16 * (((b_of - d + 15) >> 4) + n - 3 * m_of)
    seat = (2 * m_of + (p >> 7)) * 8 + ((p >> 4) & 7)
    seat = jnp.where(p < n_of, jnp.where(n < 12, seat, -1), -1)
    take_rows = lax.broadcasted_iota(jnp.int32, (layers * 8, shards * 16), 0) == seat
    take_rows = jnp.where(take_rows, 1.0, 0.0).astype(bf16)
    lane = lax.broadcasted_iota(jnp.int32, (1, shards * cap), 1)
    ids = lax.broadcasted_iota(jnp.int32, (8, shards * cap), 0) * 16 + (s % 2) * 128 + d
    batch = s // 2
    spot = jnp.zeros_like(lane)
    used = jnp.zeros(lane.shape, f32)
    aims = [jnp.zeros(lane.shape, f32) for _ in range(heads)]
    for m in range(micro):
        b, e, first_lane = jnp.zeros_like(lane), jnp.zeros_like(lane), jnp.zeros_like(lane)
        for i in range(shards):
            b = jnp.where(lane >= i * cap, begin[m][i], b)
            e = jnp.where(lane >= i * cap, length[m][i], e)
            first_lane = jnp.where(lane >= i * cap, i * cap, first_lane)
        row = lane - first_lane
        row = jnp.where(row < e, b + row, -1)
        spot = jnp.where(batch == m, row, spot)
        used = jnp.where(batch == m, mask_ref[m : m + 1, :].astype(f32), used)
        for h in range(heads):
            aim = old_ref[h, m : m + 1, :] + adv_ref[h, m : m + 1, :]
            aims[h] = jnp.where(batch == m, aim, aims[h])
    lane = lax.broadcasted_iota(jnp.int32, (1, shards * rows), 1)
    b_of, n_of, src = jnp.zeros_like(lane), jnp.zeros_like(lane), jnp.zeros_like(lane)
    for i in range(shards):
        src = jnp.where(lane >= i * rows, i, src)
    for m in range(micro):
        b, e = jnp.zeros_like(lane), jnp.zeros_like(lane)
        for i in range(shards):
            b = jnp.where(src == i, begin[m][i] + 256 * m, b)
            e = jnp.where(src == i, length[m][i], e)
        b_of = jnp.where((lane & 3) == m, b, b_of)
        n_of = jnp.where((lane & 3) == m, e, n_of)
    row = (lane - src * rows) >> 2
    tokens_at[...] = jnp.where(row < n_of, b_of + row, -1)
    pick = ids == spot
    mask = jnp.sum(jnp.where(pick, used, 0.0), axis=1, keepdims=True)
    target = [jnp.sum(jnp.where(pick, aim, 0.0), axis=1, keepdims=True) for aim in aims]

    square = jnp.zeros((rows, 128), f32)
    sums[...] = jnp.zeros(sums.shape, f32)
    est[...] = jnp.zeros(est.shape, f32)
    terms[...] = jnp.zeros(terms.shape, f32)
    for copy in loads:
        copy.wait()

    def chunk(k, square):
        cut = pl.ds(pl.multiple_of(k * part, part), part)
        x = hid_ref[:, :, cut].astype(f32).reshape(rows, part)
        left = final_ref[:, cut] * head_ref[:, cut]
        for t in range(3):
            term = left.astype(bf16).astype(f32)
            terms[8 * t : 8 * t + heads, :] = term
            left = left - term
        for i in range(part // 128):
            piece = x[:, i * 128 : (i + 1) * 128]
            square = square + piece * piece
        lines = terms[...].astype(bf16)
        x16 = x.astype(bf16)
        both = jnp.concatenate([x16, lines], axis=0)
        sums[:rows, :adapt] += mm((x * gain_ref[:, cut]).astype(bf16), win[k])
        sums[:, adapt : 2 * adapt] += mm(both, wout[k], NT)
        est[...] += mm(x16, lines, NT)
        return square

    square = lax.fori_loop(0, chunks // 2, chunk, square)
    wo_ring.relay()
    square = lax.fori_loop(chunks // 2, chunks, chunk, square)
    square = jnp.sum(square, axis=1, keepdims=True)
    gw_own = (win[d].astype(f32).T * gain_ref[:, columns]).astype(bf16)
    gw_all[y, c] = gw_own
    lane = lax.broadcasted_iota(jnp.int32, (rows, 128), 1)
    dots = [square]
    for h in range(heads):
        dots.append(est[:, h : h + 1] + est[:, 8 + h : 9 + h] + est[:, 16 + h : 17 + h])
    own_side = jnp.zeros((rows, 128), f32)
    for k, v in enumerate(dots):
        high = v.astype(bf16).astype(f32)
        own_side = jnp.where(lane == k, high, own_side)
        own_side = jnp.where(lane == len(dots) + k, v - high, own_side)
    ab = jnp.concatenate([sums[:rows, :], own_side], axis=1).astype(bf16)
    rb[...] = mm(put_rows, ab).astype(bf16).reshape(rb.shape)

    row_ids = [new() for _ in range(shards)]
    for off in range(1, shards):
        to = shard_at(off)
        send(rb.at[to], rr.at[d], row_ids[off], {"section": s, "dp": to})
    rr[d] = rb[d]

    wo_ring.finish()
    wo_ring.twins()
    gw_ring.start()

    wo_own = wo_all[y, c]
    for j in range(layers):
        rhs = jnp.where(j < s, gw_own, wo_own)
        tile = mm(wo_all[j // 2, j % 2], rhs, NT).astype(bf16)
        tp[:, :, :, j * adapt : (j + 1) * adapt] = tile.reshape(SIDE, SIDE, shards, adapt)

    mid = layers * adapt // 2
    first = {}
    for off in (2, 1, 3):
        for n, axis in enumerate(("x", "z")):
            first[n, off] = new()
            to = step(axis, off)
            cut = pl.ds(n * mid, mid)
            src = tp.at[:, to, :, cut] if n == 0 else tp.at[to, :, :, cut]
            send(src, r1.at[n, off - 1], first[n, off], peer(axis, off))
    for off in range(1, shards):
        arrived(rr.at[shard_at(-off)], row_ids[off])
    tokens = mm(take_rows, rr[...].reshape(shards * rr.shape[1], rr.shape[2]))
    own = tokens.shape[0] // layers
    lines = []
    for h in range(heads):
        at = rows + h
        lines.append(sum(sums[at + 8 * t : at + 8 * t + 1, adapt:] for t in range(3)))
    for k in range(layers):
        sb[k, :own] = tokens[k * own : (k + 1) * own]
        sb[k, own : 2 * own, :] = jnp.zeros((own, sb.shape[2]), f32)
        for h in range(heads):
            sb[k, own + h : own + h + 1, :adapt] = lines[h]
    token_ids = [new() for _ in range(layers)]
    for off in range(1, layers):
        to = layer_at(off)
        send(sb.at[to], rq.at[s], token_ids[off], {"section": to, "dp": d})
    rq[s] = sb[s]
    second = {}
    for n in (0, 1):
        kept = tp[:, x, :, :mid] if n == 0 else tp[z, :, :, mid:]
        kept = kept.astype(f32)
        for off in (1, 3, 2):
            arrived(r1.at[n, off - 1], first[n, off])
            kept = kept + r1[n, off - 1].astype(f32)
        s1[n] = kept.astype(bf16)
        axis = ("z", "x")[n]
        for off in (2, 1, 3):
            second[n, off] = new()
            send(s1.at[n, step(axis, off)], r2.at[n, off - 1], second[n, off], peer(axis, off))
    gw_ring.relay()
    for off in range(1, shards):
        src = x_all.at[c, shard_at(-off)]
        arrived(src, x_ids[off])
        send(src, src, x_swaps[off], twin)
    for n in (0, 1):
        kept = s1[n, me[("z", "x")[n]]].astype(f32)
        for off in (1, 3, 2):
            arrived(r2.at[n, off - 1], second[n, off])
            kept = kept + r2[n, off - 1].astype(f32)
        held[y, c, z, x, :, n * mid : (n + 1) * mid] = kept.astype(bf16)
    gather(lambda w, core, cut: held.at[w["y"], core, w["z"], w["x"], :, cut], layers * adapt)
    for off in range(1, layers):
        arrived(rq.at[layer_at(-off)], token_ids[off])

    def tile(l, j):
        return held[l // 2, l % 2, :, :, :, j * adapt : (j + 1) * adapt].reshape(adapt, adapt)

    coef = [1.0, coef_ref[0], coef_ref[1]]
    recurrence(layers, width, grad_scale, tile, rq, mask, target, coef, mine)
    swap = new()
    send(mine.at[1 - c], other, swap, twin)
    arrived(other, swap)
    a, b = mine[c], other[...]
    block[...] = jnp.concatenate([jnp.where(c == 0, a, b), jnp.where(c == 0, b, a)], axis=0).astype(
        bf16
    )
    pay[c, y, z, x] = block[...]

    def select():
        for off in range(1, shards):
            arrived(x_all.at[1 - c, shard_at(-off)], x_swaps[off])
        for copy in keep:
            copy.wait()
        quarter = x_sel.shape[1] // micro
        for h in (0, 1):
            for src in range(shards):
                block_in = x_all[h, src].astype(f32).reshape(rows, wide)
                xm[h, src * rows : (src + 1) * rows, :] = block_in.astype(bf16)
        at = lax.broadcasted_iota(jnp.int32, (quarter, 1), 0)
        token = ((at >> 3) & 1) * 128 + (at & 7) * 16 + (at >> 4)

        def batch(i, carried):
            m, h = i // 2, i % 2
            seat = jnp.where(token + m * 256 == tokens_at[...], 1.0, 0.0).astype(bf16)
            start = pl.multiple_of(m * quarter, quarter)
            x_sel[h, pl.ds(start, quarter), :] = mm(seat, xm[h]).astype(bf16)
            return carried

        lax.fori_loop(0, 2 * micro, batch, 0)

    gather(
        lambda w, core, cut: pay.at[core, w["y"], w["z"], w["x"], :, cut], block.shape[1], select
    )
    gw_ring.finish()
    gw_ring.twins()

    total = 2 * pay.shape[1] * shards * own

    def values(kind, at):
        cut = pl.ds(pl.multiple_of(at * adapt, adapt), adapt)
        return pay[kind, :, :, :, :, cut].reshape(total, adapt)

    def lanes(kind):
        return pay[kind, :, :, :, :, layers * adapt :].reshape(total, 128)

    scal = lanes(0).astype(f32) + lanes(1).astype(f32)
    lane = lax.broadcasted_iota(jnp.int32, (total, 128), 1)
    scal_t[...] = scal.T
    both_t[0] = values(0, s).T
    both_t[1] = values(1, s).T
    act_t, delta_t = both_t[0], both_t[1]
    head_sums = mm(act_t, lanes(0)) + mm(act_t, lanes(1))
    wide_t = act_t.astype(f32)

    def scaled(at):
        return (wide_t * -scal_t[pl.ds(at, 1), :]).astype(bf16)

    own_t = scaled(s)
    gfh = final_ref[:, columns] * head_ref[:, columns]
    for n in (0, 1):
        cut = slice(n * wide, (n + 1) * wide)
        out = mm(own_t, x_sel[n])
        for h in range(heads):
            out = out + head_sums[:, layers + h : layers + h + 1] * gfh[h : h + 1, cut]
        acc[0, :, cut] = out
        acc[1, :, cut] = mm(delta_t, x_sel[n])
    for j in range(layers):
        which = jnp.where(j > s, 0, 1)
        left = mm(scaled(jnp.maximum(j, s)), values(0, j)).astype(bf16)
        right = mm(both_t[which], values(1 - which, j)).astype(bf16)
        acc[0] += mm(left, wo_all[j // 2, j % 2])
        acc[jnp.where(j == s, 2, which)] += mm(right, weights[1 - which, j // 2, j % 2])
    grad_out_ref[...] = acc[0]
    grad_in_ref[...] = (acc[1] * gain_ref[:, columns]).T
    loss = jnp.sum(jnp.where(lane == layers + heads, scal, 0.0), axis=0, keepdims=True)
    loss_ref[0, 0] = jnp.sum(loss) / total
    for copy in issued:
        copy.wait_send()


def recurrence(layers, width, grad_scale, tile, rows_ref, mask, target, coef, out_ref):
    adapt = 256
    heads = len(target)
    own = mask.shape[0]
    sums = rows_ref[0, :own, 2 * adapt :]
    part = lambda k: sums[:, k : k + 1] + sums[:, 1 + heads + k : 2 + heads + k]
    sq = part(0)
    est = [part(1 + k) for k in range(heads)]
    into = [rows_ref[k, :own, :adapt] for k in range(layers)]
    onto = [rows_ref[k, :own, adapt : 2 * adapt] for k in range(layers)]
    head_out = [
        [rows_ref[k, own + h : own + h + 1, :adapt] for h in range(heads)] for k in range(layers)
    ]
    pre, fac, kept = [], [], {}
    for j in range(layers):
        f = lax.rsqrt(jnp.maximum(sq, 0.0) / width + EPS)
        p = f * into[j]
        act = (p * jax.nn.sigmoid(p)).astype(bf16)
        wide = act.astype(f32)
        out_ref[0, :, j * adapt : (j + 1) * adapt] = wide
        pre.append(p)
        fac.append(f)
        for k in range(j):
            kept[j, k] = onto[k]
        before = onto[j]
        for k in range(layers):
            if k <= j:
                onto[k] = onto[k] + mm(act, tile(k, j))
            else:
                into[k] = into[k] + mm(act, tile(k, j))
                onto[k] = onto[k] + mm(act, tile(j, k), NT)
        sq = sq + jnp.sum(wide * (before + onto[j]), axis=1, keepdims=True)
        for h in range(heads):
            est[h] = est[h] + jnp.sum(wide * head_out[j][h], axis=1, keepdims=True)
    f = lax.rsqrt(jnp.maximum(sq, 0.0) / width + EPS)
    loss = jnp.zeros_like(sq)
    along = jnp.zeros_like(sq)
    lane = lax.broadcasted_iota(jnp.int32, (own, 128), 1)
    extra = jnp.zeros(lane.shape, f32)
    grads = []
    for h in range(heads):
        e = f * est[h]
        err = e - target[h]
        weighted = coef[h] * mask * err
        loss = loss + 0.5 * weighted * err
        scaled = weighted * grad_scale
        along = along + scaled * e
        grads.append(f * scaled)
        extra = jnp.where(lane == layers + h, grads[h], extra)
    extra = jnp.where(lane == layers + heads, loss, extra)
    total = f * f * along / width
    back = []
    for k in range(layers):
        start = -total * onto[k]
        for h in range(heads):
            start = start + grads[h] * head_out[k][h]
        back.append(start)
    for l in range(layers - 1, -1, -1):
        extra = jnp.where(lane == l, total, extra)
        sg = jax.nn.sigmoid(pre[l])
        delta = (fac[l] * (back[l] * sg * (1.0 + pre[l] * (1.0 - sg)))).astype(bf16)
        wide = delta.astype(f32)
        out_ref[1, :, l * adapt : (l + 1) * adapt] = wide
        s = fac[l] / width * jnp.sum(wide * pre[l], axis=1, keepdims=True)
        total = total + s
        for k in range(l):
            back[k] = back[k] + mm(delta, tile(l, k), NT) - s * kept[l, k]
    high = extra.astype(bf16).astype(f32)
    out_ref[0, :, layers * adapt :] = high
    out_ref[1, :, layers * adapt :] = extra - high


def results(grad_in_ref, grad_out_ref, in_ref, out_ref):
    in_ref[...] = grad_in_ref[...]
    out_ref[...] = grad_out_ref[...]


def local(
    hidden,
    lengths,
    response_mask,
    norm_gain,
    weight_in,
    weight_out,
    final_gain,
    value_heads,
    old_values,
    advantages,
    multipliers,
):
    shards = lax.axis_size("dp")
    layers = lax.axis_size("section")
    micro, cap, width = hidden.shape
    heads = value_heads.shape[0]
    adapt = weight_in.shape[2]
    total = micro * BAL * shards
    part = width // shards
    own = total // (shards * layers)

    sm = pl.BlockSpec(memory_space=pltpu.SMEM)
    vm = pl.BlockSpec(memory_space=pltpu.VMEM)
    hbm = pl.BlockSpec(memory_space=pl.ANY)
    columns = layers * adapt + 128
    wide = 2 * adapt + 128
    half = layers * adapt // 2
    grad_in, grad_out, loss = pl.pallas_call(
        functools.partial(kernel, layers, float(width), LOSS_SCALE / total),
        out_shape=(
            jax.ShapeDtypeStruct((part, adapt), f32),
            jax.ShapeDtypeStruct((adapt, part), f32),
            jax.ShapeDtypeStruct((1, 1), f32),
        ),
        in_specs=[sm, sm, hbm, hbm] + [vm] * 7,
        out_specs=(vm, vm, sm),
        scratch_shapes=[
            pltpu.VMEM((shards, part, adapt), bf16),
            pltpu.VMEM((shards, adapt, part), bf16),
            pltpu.VMEM((micro * cap + 32, 2 * adapt), f32),
            pltpu.VMEM((micro * cap, 32), f32),
            pltpu.VMEM((32, part), f32),
            pltpu.VMEM((1, shards * micro * cap), jnp.int32),
            pltpu.VMEM((2, shards * micro * cap, part // 2), bf16),
            pltpu.VMEM((2, SIDE, 2, adapt, part), bf16),
            pltpu.VMEM((2, shards, cap, micro, part // 2), bf16),
            pltpu.VMEM((2, total, part // 2), bf16),
            pltpu.VMEM((2, SIDE, SIDE, SIDE, 16, columns), bf16),
            pltpu.VMEM((shards, 16, wide), bf16),
            pltpu.VMEM((SIDE, SIDE, 16, layers * adapt), bf16),
            pltpu.VMEM((2, 3, SIDE, 16, half), bf16),
            pltpu.VMEM((2, SIDE, 16, half), bf16),
            pltpu.VMEM((2, 3, 16, half), bf16),
            pltpu.VMEM((SIDE, 2, SIDE, SIDE, 16, layers * adapt), bf16),
            pltpu.VMEM((shards, 16, wide), bf16),
            pltpu.VMEM((layers, 2 * own, wide), f32),
            pltpu.VMEM((layers, 2 * own, wide), f32),
            pltpu.VMEM((2, own, columns), f32),
            pltpu.VMEM((own, columns), f32),
            pltpu.VMEM((16, columns), bf16),
            pltpu.VMEM((3, adapt, part), f32),
            pltpu.VMEM((2, adapt, total), bf16),
            pltpu.VMEM((128, total), f32),
            pltpu.SemaphoreType.DMA((COPIES,)),
            pltpu.SemaphoreType.DMA((COPIES,)),
            pltpu.SemaphoreType.DMA((40,)),
        ],
        compiler_params=pltpu.CompilerParams(
            vmem_limit_bytes=60 * 1024 * 1024, collective_id=0, has_side_effects=True
        ),
        cost_estimate=pl.CostEstimate(
            flops=10**10, bytes_accessed=3 * 10**7, transcendentals=0
        ),
        name="layers",
    )(
        lengths,
        multipliers,
        weight_in[0],
        weight_out[0],
        norm_gain,
        jnp.swapaxes(hidden, 0, 1),
        final_gain[None],
        value_heads,
        response_mask,
        old_values,
        advantages,
    )
    grad_in, grad_out = pl.pallas_call(
        results,
        out_shape=(
            jax.ShapeDtypeStruct(grad_in.shape, f32),
            jax.ShapeDtypeStruct(grad_out.shape, f32),
        ),
        in_specs=[vm, vm],
        out_specs=(vm, vm),
        name="results",
    )(grad_in, grad_out)
    return (grad_in[None], grad_out[None], loss[0, 0])


def solution(mesh):
    return jax.shard_map(
        local,
        mesh=mesh,
        in_specs=(
            P(None, "dp", None),
            P(),
            P(),
            P("section", None),
            P("section", None, None),
            P("section", None, None),
            P(),
            P(),
            P(),
            P(),
            P(),
        ),
        out_specs=(P("section", "dp", None), P("section", None, "dp"), P()),
        check_vma=False,
    )
```

```python
import functools

import jax
import jax.numpy as jnp
from jax import lax
from jax.experimental import pallas as pl
from jax.experimental.pallas import tpu as pltpu
from jax.sharding import PartitionSpec as P

EPS = 1e-05
LOSS_SCALE = 4096.0
BAL = 16

f32 = jnp.float32
bf16 = jnp.bfloat16
NT = (((1,), (1,)), ((), ()))
TN = (((0,), (0,)), ((), ()))
NN = (((1,), (0,)), ((), ()))
MESH = pl.DeviceIdType.MESH
SIDE = 4
COPIES = 360


def mm(a, b, dims=NN):
    return lax.dot_general(a, b, dims, preferred_element_type=f32)


def kernel(
    layers,
    width,
    grad_scale,
    lengths_ref,
    coef_ref,
    win_ref,
    wout_ref,
    gain_in,
    hid_in,
    final_in,
    head_in,
    mask_in,
    old_in,
    adv_in,
    grad_in_ref,
    grad_out_ref,
    loss_ref,
    gain_ref,
    hid_ref,
    final_ref,
    head_ref,
    mask_ref,
    old_ref,
    adv_ref,
    win,
    wout,
    sums,
    est,
    terms,
    tokens_at,
    xm,
    weights,
    x_all,
    x_sel,
    pay,
    rb,
    tp,
    r1,
    s1,
    r2,
    held,
    rr,
    sb,
    rq,
    mine,
    other,
    block,
    acc,
    both_t,
    scal_t,
    send_sem,
    recv_sem,
    local_sem,
):
    s = lax.axis_index("section")
    d = lax.axis_index("dp")
    y, c = s // 2, s % 2
    z, x = d // SIDE, d % SIDE
    me = {"x": x, "y": y, "z": z}
    shards = SIDE * SIDE
    chunks, part, adapt = win.shape
    heads = head_ref.shape[0]
    cap, micro = hid_ref.shape[:2]
    rows = micro * cap
    step = lambda a, off: (me[a] + off + SIDE) % SIDE

    def peer(axis, off):
        if axis == "x":
            return {"section": s, "dp": z * SIDE + step("x", off)}
        if axis == "z":
            return {"section": s, "dp": step("z", off) * SIDE + x}
        return {"section": step("y", off) * 2 + c, "dp": d}

    twin = {"section": y * 2 + (1 - c), "dp": d}

    def shard_at(off):
        return (d + off + shards) % shards

    def layer_at(off):
        return (s + off + layers) % layers

    issued = []
    count = [0, 0]

    def new():
        count[0] += 1
        return count[0] - 1

    def remote(src, dst, at, to):
        return pltpu.make_async_remote_copy(
            src_ref=src,
            dst_ref=dst,
            send_sem=send_sem.at[at],
            recv_sem=recv_sem.at[at],
            device_id=to,
            device_id_type=MESH,
        )

    def send(src, dst, at, to):
        copy = remote(src, dst, at, to)
        copy.start()
        issued.append(copy)

    def arrived(dst, at):
        remote(dst, dst, at, twin).wait_recv()

    def local(src, dst):
        count[1] += 1
        copy = pltpu.make_async_copy(src, dst, local_sem.at[count[1] - 1])
        copy.start()
        return copy

    class Ring:
        def __init__(self, axis, slab, swaps=False):
            self.slab = slab
            self.ids = [new() for _ in range(6)]
            self.plus, self.minus = peer(axis, 1), peer(axis, -1)
            self.swaps = {}
            if swaps:
                for v in (0, -1, 1, 2):
                    for h in (0, 1):
                        self.swaps[v, h] = new()

        def send(self, v, h, n, to):
            ref = self.slab(v, h, c)
            send(ref, ref, self.ids[n], to)

        def wait(self, v, h, n):
            arrived(self.slab(v, h, c), self.ids[n])
            self.swap(v, h)

        def swap(self, v, h):
            if self.swaps:
                ref = self.slab(v, h, c)
                send(ref, ref, self.swaps[v, h], twin)

        def start(self):
            self.send(0, 0, 0, self.plus)
            self.send(0, 1, 2, self.minus)
            self.send(0, 1, 1, self.plus)
            self.send(0, 0, 3, self.minus)
            self.swap(0, 0)
            self.swap(0, 1)

        def relay(self):
            arrived(self.slab(-1, 0, c), self.ids[0])
            self.send(-1, 0, 4, self.plus)
            arrived(self.slab(1, 1, c), self.ids[2])
            self.send(1, 1, 5, self.minus)
            self.swap(-1, 0)
            self.swap(1, 1)

        def finish(self):
            self.wait(-1, 1, 1)
            self.wait(1, 0, 3)
            self.wait(2, 0, 4)
            self.wait(2, 1, 5)

        def twins(self):
            for (v, h), at in self.swaps.items():
                arrived(self.slab(v, h, 1 - c), at)

    def gather(at, columns, meanwhile=None):
        third = (columns + 192) // 384 * 128
        bounds = [0, third, 2 * third, columns]
        orders = [("x", "z", "y"), ("z", "y", "x"), ("y", "x", "z")]
        parts = range(3)

        def ref(p, core, *steps):
            where = {
                axis: pl.ds(0, SIDE) if v is None else step(axis, v)
                for axis, v in zip(orders[p], steps)
            }
            return at(where, core, pl.ds(bounds[p], bounds[p + 1] - bounds[p]))

        ids, swaps = {}, {}

        def put(at_, block, to):
            ids[at_] = new()
            send(block, block, ids[at_], to)

        def swap(p, row, v):
            swaps[p, row, v] = new()
            block = ref(p, c, None, row, v)
            send(block, block, swaps[p, row, v], twin)

        def ring(p, row):
            axis = orders[p][2]
            for off in (1, -1):
                put((p, row, off), ref(p, c, None, row, 0), peer(axis, off))
            swap(p, row, 0)

        way = {0: 1, -1: -1, -3: 1, -2: -1}

        def relay(p, row):
            g = way[row]
            block = ref(p, c, None, row, -g)
            arrived(block, ids[p, row, g])
            put((p, row, 2), block, peer(orders[p][2], g))
            swap(p, row, -g)

        def end(p, row, v, n):
            arrived(ref(p, c, None, row, v), ids[p, row, n])
            swap(p, row, v)

        for off in (2, 1, 3):
            for p in parts:
                put((0, p, off, "a"), ref(p, c, 0, 0, 0), peer(orders[p][0], off))
        for off in (1, 3, 2):
            for p in parts:
                arrived(ref(p, c, -off, 0, 0), ids[0, p, off, "a"])
        for off in (2, 1, 3):
            for p in parts:
                put((1, p, off, "b"), ref(p, c, None, 0, 0), peer(orders[p][1], off))
        for p in parts:
            ring(p, 0)
        for off in (1, 3):
            for p in parts:
                arrived(ref(p, c, None, -off, 0), ids[1, p, off, "b"])
                ring(p, -off)
        for p in parts:
            relay(p, 0)
        for p in parts:
            arrived(ref(p, c, None, -2, 0), ids[1, p, 2, "b"])
            ring(p, -2)
        if meanwhile is not None:
            meanwhile()
        order = (0, -1, -3, -2)
        for row in order[1:]:
            for p in parts:
                relay(p, row)
        for row in order:
            for p in parts:
                end(p, row, way[row], -way[row])
        for row in order:
            for p in parts:
                end(p, row, 2, 2)
        for (p, row, v), at_ in swaps.items():
            arrived(ref(p, 1 - c, None, row, v), at_)

    wo_all, gw_all = weights.at[0], weights.at[1]
    columns = pl.ds(pl.multiple_of(d * part, part), part)
    own_wo = local(wout_ref.at[:, columns], wo_all.at[y, c])
    own_hid = local(hid_in, hid_ref)
    small = [
        local(src, dst)
        for src, dst in (
            (gain_in, gain_ref),
            (final_in, final_ref),
            (head_in, head_ref),
            (mask_in, mask_ref),
            (old_in, old_ref),
            (adv_in, adv_ref),
        )
    ]
    loads = []
    for k in range(chunks):
        loads.append(local(win_ref.at[pl.ds(k * part, part)], win.at[k]))
        loads.append(local(wout_ref.at[:, pl.ds(k * part, part)], wout.at[k]))

    barrier = pltpu.get_barrier_semaphore()
    for off in range(1, shards):
        pl.semaphore_signal(
            barrier, inc=1, device_id={"section": s, "dp": shard_at(off)}, device_id_type=MESH
        )
    for off in range(1, layers):
        pl.semaphore_signal(
            barrier, inc=1, device_id={"section": layer_at(off), "dp": d}, device_id_type=MESH
        )
    pl.semaphore_wait(barrier, shards + layers - 2)

    half = adapt // 2
    wo_ring = Ring(
        "y", lambda v, h, core: wo_all.at[step("y", v), core, pl.ds(h * half, half)], True
    )
    own_wo.wait()
    wo_ring.start()
    own_hid.wait()
    wide = part // 2
    keep = []
    for h in (0, 1):
        keep.append(
            local(
                hid_ref.at[:, :, pl.ds(pl.multiple_of(d * part + h * wide, wide), wide)],
                x_all.at[h, d],
            )
        )
    x_ids = [new() for _ in range(shards)]
    x_swaps = [new() for _ in range(shards)]
    for off in range(1, shards):
        to = shard_at(off)
        send(
            hid_ref.at[:, :, pl.ds(pl.multiple_of(to * part + c * wide, wide), wide)],
            x_all.at[c, d],
            x_ids[off],
            {"section": s, "dp": to},
        )
    gw_ring = Ring(
        "y", lambda v, h, core: gw_all.at[step("y", v), core, pl.ds(h * half, half)], True
    )

    for copy in small:
        copy.wait()

    begin = [[None] * shards for _ in range(micro)]
    length = [[lengths_ref[m, i] for i in range(shards)] for m in range(micro)]
    mine_at = []
    for m in range(micro):
        at, here = jnp.int32(0), jnp.int32(0)
        for i in range(shards):
            begin[m][i] = at
            here = here + jnp.where(i < d, length[m][i], 0)
            at = at + length[m][i]
        mine_at.append(here)
    lane = lax.broadcasted_iota(jnp.int32, (1, rows), 1)
    b_of, n_of = jnp.zeros_like(lane), jnp.zeros_like(lane)
    m_of, r_of = lane & 3, lane >> 2
    for m in range(micro):
        b_of = jnp.where(m_of == m, mine_at[m], b_of)
        n_of = jnp.where(m_of == m, lengths_ref[m, d], n_of)
    p = b_of + r_of
    n = (p >> 4) - ((b_of - (p & 15) + 15) >> 4)
    slot = jnp.where(r_of < n_of, (p & 15) * 16 + m_of * 3 + n, -1)
    put_rows = lax.broadcasted_iota(jnp.int32, (shards * 16, rows), 0) == slot
    put_rows = jnp.where(put_rows, 1.0, 0.0).astype(bf16)
    lane = lax.broadcasted_iota(jnp.int32, (1, shards * 16), 1)
    src, n = lane >> 4, lane & 15
    m_of = jnp.where(n >= 3, 1, 0) + jnp.where(n >= 6, 1, 0) + jnp.where(n >= 9, 1, 0)
    b_of, n_of = jnp.zeros_like(lane), jnp.zeros_like(lane)
    for m in range(micro):
        b, e = jnp.zeros_like(lane), jnp.zeros_like(lane)
        for i in range(shards):
            b = jnp.where(src == i, begin[m][i], b)
            e = jnp.where(src == i, begin[m][i] + length[m][i], e)
        b_of = jnp.where(m_of == m, b, b_of)
        n_of = jnp.where(m_of == m, e, n_of)
    p = d + 16 * (((b_of - d + 15) >> 4) + n - 3 * m_of)
    seat = (2 * m_of + (p >> 7)) * 8 + ((p >> 4) & 7)
    seat = jnp.where(p < n_of, jnp.where(n < 12, seat, -1), -1)
    take_rows = lax.broadcasted_iota(jnp.int32, (layers * 8, shards * 16), 0) == seat
    take_rows = jnp.where(take_rows, 1.0, 0.0).astype(bf16)
    lane = lax.broadcasted_iota(jnp.int32, (1, shards * cap), 1)
    ids = lax.broadcasted_iota(jnp.int32, (8, shards * cap), 0) * 16 + (s % 2) * 128 + d
    batch = s // 2
    spot = jnp.zeros_like(lane)
    used = jnp.zeros(lane.shape, f32)
    aims = [jnp.zeros(lane.shape, f32) for _ in range(heads)]
    for m in range(micro):
        b, e, first_lane = jnp.zeros_like(lane), jnp.zeros_like(lane), jnp.zeros_like(lane)
        for i in range(shards):
            b = jnp.where(lane >= i * cap, begin[m][i], b)
            e = jnp.where(lane >= i * cap, length[m][i], e)
            first_lane = jnp.where(lane >= i * cap, i * cap, first_lane)
        row = lane - first_lane
        row = jnp.where(row < e, b + row, -1)
        spot = jnp.where(batch == m, row, spot)
        used = jnp.where(batch == m, mask_ref[m : m + 1, :].astype(f32), used)
        for h in range(heads):
            aim = old_ref[h, m : m + 1, :] + adv_ref[h, m : m + 1, :]
            aims[h] = jnp.where(batch == m, aim, aims[h])
    lane = lax.broadcasted_iota(jnp.int32, (1, shards * rows), 1)
    b_of, n_of, src = jnp.zeros_like(lane), jnp.zeros_like(lane), jnp.zeros_like(lane)
    for i in range(shards):
        src = jnp.where(lane >= i * rows, i, src)
    for m in range(micro):
        b, e = jnp.zeros_like(lane), jnp.zeros_like(lane)
        for i in range(shards):
            b = jnp.where(src == i, begin[m][i] + 256 * m, b)
            e = jnp.where(src == i, length[m][i], e)
        b_of = jnp.where((lane & 3) == m, b, b_of)
        n_of = jnp.where((lane & 3) == m, e, n_of)
    row = (lane - src * rows) >> 2
    tokens_at[...] = jnp.where(row < n_of, b_of + row, -1)
    pick = ids == spot
    mask = jnp.sum(jnp.where(pick, used, 0.0), axis=1, keepdims=True)
    target = [jnp.sum(jnp.where(pick, aim, 0.0), axis=1, keepdims=True) for aim in aims]

    square = jnp.zeros((rows, 128), f32)
    sums[...] = jnp.zeros(sums.shape, f32)
    est[...] = jnp.zeros(est.shape, f32)
    terms[...] = jnp.zeros(terms.shape, f32)
    for copy in loads:
        copy.wait()

    def chunk(k, square):
        cut = pl.ds(pl.multiple_of(k * part, part), part)
        x = hid_ref[:, :, cut].astype(f32).reshape(rows, part)
        left = final_ref[:, cut] * head_ref[:, cut]
        for t in range(3):
            term = left.astype(bf16).astype(f32)
            terms[8 * t : 8 * t + heads, :] = term
            left = left - term
        for i in range(part // 128):
            piece = x[:, i * 128 : (i + 1) * 128]
            square = square + piece * piece
        lines = terms[...].astype(bf16)
        x16 = x.astype(bf16)
        both = jnp.concatenate([x16, lines], axis=0)
        sums[:rows, :adapt] += mm((x * gain_ref[:, cut]).astype(bf16), win[k])
        sums[:, adapt : 2 * adapt] += mm(both, wout[k], NT)
        est[...] += mm(x16, lines, NT)
        return square

    square = lax.fori_loop(0, chunks // 2, chunk, square)
    wo_ring.relay()
    square = lax.fori_loop(chunks // 2, chunks, chunk, square)
    square = jnp.sum(square, axis=1, keepdims=True)
    gw_own = (win[d].astype(f32).T * gain_ref[:, columns]).astype(bf16)
    gw_all[y, c] = gw_own
    lane = lax.broadcasted_iota(jnp.int32, (rows, 128), 1)
    dots = [square]
    for h in range(heads):
        dots.append(est[:, h : h + 1] + est[:, 8 + h : 9 + h] + est[:, 16 + h : 17 + h])
    own_side = jnp.zeros((rows, 128), f32)
    for k, v in enumerate(dots):
        high = v.astype(bf16).astype(f32)
        own_side = jnp.where(lane == k, high, own_side)
        own_side = jnp.where(lane == len(dots) + k, v - high, own_side)
    ab = jnp.concatenate([sums[:rows, :], own_side], axis=1).astype(bf16)
    rb[...] = mm(put_rows, ab).astype(bf16).reshape(rb.shape)

    row_ids = [new() for _ in range(shards)]
    for off in range(1, shards):
        to = shard_at(off)
        send(rb.at[to], rr.at[d], row_ids[off], {"section": s, "dp": to})
    rr[d] = rb[d]

    wo_ring.finish()
    wo_ring.twins()
    gw_ring.start()

    wo_own = wo_all[y, c]
    for j in range(layers):
        rhs = jnp.where(j < s, gw_own, wo_own)
        tile = mm(wo_all[j // 2, j % 2], rhs, NT).astype(bf16)
        tp[:, :, :, j * adapt : (j + 1) * adapt] = tile.reshape(SIDE, SIDE, shards, adapt)

    mid = layers * adapt // 2
    first = {}
    for off in (2, 1, 3):
        for n, axis in enumerate(("x", "z")):
            first[n, off] = new()
            to = step(axis, off)
            cut = pl.ds(n * mid, mid)
            src = tp.at[:, to, :, cut] if n == 0 else tp.at[to, :, :, cut]
            send(src, r1.at[n, off - 1], first[n, off], peer(axis, off))
    for off in range(1, shards):
        arrived(rr.at[shard_at(-off)], row_ids[off])
    tokens = mm(take_rows, rr[...].reshape(shards * rr.shape[1], rr.shape[2]))
    own = tokens.shape[0] // layers
    lines = []
    for h in range(heads):
        at = rows + h
        lines.append(sum(sums[at + 8 * t : at + 8 * t + 1, adapt:] for t in range(3)))
    for k in range(layers):
        sb[k, :own] = tokens[k * own : (k + 1) * own]
        sb[k, own : 2 * own, :] = jnp.zeros((own, sb.shape[2]), f32)
        for h in range(heads):
            sb[k, own + h : own + h + 1, :adapt] = lines[h]
    token_ids = [new() for _ in range(layers)]
    for off in range(1, layers):
        to = layer_at(off)
        send(sb.at[to], rq.at[s], token_ids[off], {"section": to, "dp": d})
    rq[s] = sb[s]
    second = {}
    for n in (0, 1):
        kept = tp[:, x, :, :mid] if n == 0 else tp[z, :, :, mid:]
        kept = kept.astype(f32)
        for off in (1, 3, 2):
            arrived(r1.at[n, off - 1], first[n, off])
            kept = kept + r1[n, off - 1].astype(f32)
        s1[n] = kept.astype(bf16)
        axis = ("z", "x")[n]
        for off in (2, 1, 3):
            second[n, off] = new()
            send(s1.at[n, step(axis, off)], r2.at[n, off - 1], second[n, off], peer(axis, off))
    gw_ring.relay()
    for off in range(1, shards):
        src = x_all.at[c, shard_at(-off)]
        arrived(src, x_ids[off])
        send(src, src, x_swaps[off], twin)
    for n in (0, 1):
        kept = s1[n, me[("z", "x")[n]]].astype(f32)
        for off in (1, 3, 2):
            arrived(r2.at[n, off - 1], second[n, off])
            kept = kept + r2[n, off - 1].astype(f32)
        held[y, c, z, x, :, n * mid : (n + 1) * mid] = kept.astype(bf16)
    gather(lambda w, core, cut: held.at[w["y"], core, w["z"], w["x"], :, cut], layers * adapt)
    for off in range(1, layers):
        arrived(rq.at[layer_at(-off)], token_ids[off])

    def tile(l, j):
        return held[l // 2, l % 2, :, :, :, j * adapt : (j + 1) * adapt].reshape(adapt, adapt)

    coef = [1.0, coef_ref[0], coef_ref[1]]
    recurrence(layers, width, grad_scale, tile, rq, mask, target, coef, mine)
    swap = new()
    send(mine.at[1 - c], other, swap, twin)
    arrived(other, swap)
    a, b = mine[c], other[...]
    block[...] = jnp.concatenate([jnp.where(c == 0, a, b), jnp.where(c == 0, b, a)], axis=0).astype(
        bf16
    )
    pay[c, y, z, x] = block[...]

    def select():
        for off in range(1, shards):
            arrived(x_all.at[1 - c, shard_at(-off)], x_swaps[off])
        for copy in keep:
            copy.wait()
        quarter = x_sel.shape[1] // micro
        for h in (0, 1):
            for src in range(shards):
                block_in = x_all[h, src].astype(f32).reshape(rows, wide)
                xm[h, src * rows : (src + 1) * rows, :] = block_in.astype(bf16)
        at = lax.broadcasted_iota(jnp.int32, (quarter, 1), 0)
        token = ((at >> 3) & 1) * 128 + (at & 7) * 16 + (at >> 4)

        def batch(i, carried):
            m, h = i // 2, i % 2
            seat = jnp.where(token + m * 256 == tokens_at[...], 1.0, 0.0).astype(bf16)
            start = pl.multiple_of(m * quarter, quarter)
            x_sel[h, pl.ds(start, quarter), :] = mm(seat, xm[h]).astype(bf16)
            return carried

        lax.fori_loop(0, 2 * micro, batch, 0)

    gather(
        lambda w, core, cut: pay.at[core, w["y"], w["z"], w["x"], :, cut], block.shape[1], select
    )
    gw_ring.finish()
    gw_ring.twins()

    total = 2 * pay.shape[1] * shards * own

    def values(kind, at):
        cut = pl.ds(pl.multiple_of(at * adapt, adapt), adapt)
        return pay[kind, :, :, :, :, cut].reshape(total, adapt)

    def lanes(kind):
        return pay[kind, :, :, :, :, layers * adapt :].reshape(total, 128)

    scal = lanes(0).astype(f32) + lanes(1).astype(f32)
    lane = lax.broadcasted_iota(jnp.int32, (total, 128), 1)
    scal_t[...] = scal.T
    both_t[0] = values(0, s).T
    both_t[1] = values(1, s).T
    act_t, delta_t = both_t[0], both_t[1]
    head_sums = mm(act_t, lanes(0)) + mm(act_t, lanes(1))
    wide_t = act_t.astype(f32)

    def scaled(at):
        return (wide_t * -scal_t[pl.ds(at, 1), :]).astype(bf16)

    own_t = scaled(s)
    gfh = final_ref[:, columns] * head_ref[:, columns]
    for n in (0, 1):
        cut = slice(n * wide, (n + 1) * wide)
        out = mm(own_t, x_sel[n])
        for h in range(heads):
            out = out + head_sums[:, layers + h : layers + h + 1] * gfh[h : h + 1, cut]
        acc[0, :, cut] = out
        acc[1, :, cut] = mm(delta_t, x_sel[n])
    for j in range(layers):
        which = jnp.where(j > s, 0, 1)
        left = mm(scaled(jnp.maximum(j, s)), values(0, j)).astype(bf16)
        right = mm(both_t[which], values(1 - which, j)).astype(bf16)
        acc[0] += mm(left, wo_all[j // 2, j % 2])
        acc[jnp.where(j == s, 2, which)] += mm(right, weights[1 - which, j // 2, j % 2])
    grad_out_ref[...] = acc[0]
    grad_in_ref[...] = (acc[1] * gain_ref[:, columns]).T
    loss = jnp.sum(jnp.where(lane == layers + heads, scal, 0.0), axis=0, keepdims=True)
    loss_ref[0, 0] = jnp.sum(loss) / total
    for copy in issued:
        copy.wait_send()


def recurrence(layers, width, grad_scale, tile, rows_ref, mask, target, coef, out_ref):
    adapt = 256
    heads = len(target)
    own = mask.shape[0]
    sums = rows_ref[0, :own, 2 * adapt :]
    part = lambda k: sums[:, k : k + 1] + sums[:, 1 + heads + k : 2 + heads + k]
    sq = part(0)
    est = [part(1 + k) for k in range(heads)]
    into = [rows_ref[k, :own, :adapt] for k in range(layers)]
    onto = [rows_ref[k, :own, adapt : 2 * adapt] for k in range(layers)]
    head_out = [
        [rows_ref[k, own + h : own + h + 1, :adapt] for h in range(heads)] for k in range(layers)
    ]
    pre, fac, kept = [], [], {}
    for j in range(layers):
        f = lax.rsqrt(jnp.maximum(sq, 0.0) / width + EPS)
        p = f * into[j]
        act = (p * jax.nn.sigmoid(p)).astype(bf16)
        wide = act.astype(f32)
        out_ref[0, :, j * adapt : (j + 1) * adapt] = wide
        pre.append(p)
        fac.append(f)
        for k in range(j):
            kept[j, k] = onto[k]
        before = onto[j]
        for k in range(layers):
            if k <= j:
                onto[k] = onto[k] + mm(act, tile(k, j))
            else:
                into[k] = into[k] + mm(act, tile(k, j))
                onto[k] = onto[k] + mm(act, tile(j, k), NT)
        sq = sq + jnp.sum(wide * (before + onto[j]), axis=1, keepdims=True)
        for h in range(heads):
            est[h] = est[h] + jnp.sum(wide * head_out[j][h], axis=1, keepdims=True)
    f = lax.rsqrt(jnp.maximum(sq, 0.0) / width + EPS)
    loss = jnp.zeros_like(sq)
    along = jnp.zeros_like(sq)
    lane = lax.broadcasted_iota(jnp.int32, (own, 128), 1)
    extra = jnp.zeros(lane.shape, f32)
    grads = []
    for h in range(heads):
        e = f * est[h]
        err = e - target[h]
        weighted = coef[h] * mask * err
        loss = loss + 0.5 * weighted * err
        scaled = weighted * grad_scale
        along = along + scaled * e
        grads.append(f * scaled)
        extra = jnp.where(lane == layers + h, grads[h], extra)
    extra = jnp.where(lane == layers + heads, loss, extra)
    total = f * f * along / width
    back = []
    for k in range(layers):
        start = -total * onto[k]
        for h in range(heads):
            start = start + grads[h] * head_out[k][h]
        back.append(start)
    for l in range(layers - 1, -1, -1):
        extra = jnp.where(lane == l, total, extra)
        sg = jax.nn.sigmoid(pre[l])
        delta = (fac[l] * (back[l] * sg * (1.0 + pre[l] * (1.0 - sg)))).astype(bf16)
        wide = delta.astype(f32)
        out_ref[1, :, l * adapt : (l + 1) * adapt] = wide
        s = fac[l] / width * jnp.sum(wide * pre[l], axis=1, keepdims=True)
        total = total + s
        for k in range(l):
            back[k] = back[k] + mm(delta, tile(l, k), NT) - s * kept[l, k]
    high = extra.astype(bf16).astype(f32)
    out_ref[0, :, layers * adapt :] = high
    out_ref[1, :, layers * adapt :] = extra - high


def results(grad_in_ref, grad_out_ref, in_ref, out_ref):
    in_ref[...] = grad_in_ref[...]
    out_ref[...] = grad_out_ref[...]


def local(
    hidden,
    lengths,
    response_mask,
    norm_gain,
    weight_in,
    weight_out,
    final_gain,
    value_heads,
    old_values,
    advantages,
    multipliers,
):
    shards = lax.axis_size("dp")
    layers = lax.axis_size("section")
    micro, cap, width = hidden.shape
    heads = value_heads.shape[0]
    adapt = weight_in.shape[2]
    total = micro * BAL * shards
    part = width // shards
    own = total // (shards * layers)

    sm = pl.BlockSpec(memory_space=pltpu.SMEM)
    vm = pl.BlockSpec(memory_space=pltpu.VMEM)
    hbm = pl.BlockSpec(memory_space=pl.ANY)
    columns = layers * adapt + 128
    wide = 2 * adapt + 128
    half = layers * adapt // 2
    grad_in, grad_out, loss = pl.pallas_call(
        functools.partial(kernel, layers, float(width), LOSS_SCALE / total),
        out_shape=(
            jax.ShapeDtypeStruct((part, adapt), f32),
            jax.ShapeDtypeStruct((adapt, part), f32),
            jax.ShapeDtypeStruct((1, 1), f32),
        ),
        in_specs=[sm, sm] + [hbm] * 9,
        out_specs=(vm, vm, sm),
        scratch_shapes=[
            pltpu.VMEM((1, width), f32),
            pltpu.VMEM((cap, micro, width), bf16),
            pltpu.VMEM((1, width), f32),
            pltpu.VMEM((heads, width), f32),
            pltpu.VMEM(response_mask.shape, jnp.int32),
            pltpu.VMEM(old_values.shape, f32),
            pltpu.VMEM(advantages.shape, f32),
            pltpu.VMEM((shards, part, adapt), bf16),
            pltpu.VMEM((shards, adapt, part), bf16),
            pltpu.VMEM((micro * cap + 32, 2 * adapt), f32),
            pltpu.VMEM((micro * cap, 32), f32),
            pltpu.VMEM((32, part), f32),
            pltpu.VMEM((1, shards * micro * cap), jnp.int32),
            pltpu.VMEM((2, shards * micro * cap, part // 2), bf16),
            pltpu.VMEM((2, SIDE, 2, adapt, part), bf16),
            pltpu.VMEM((2, shards, cap, micro, part // 2), bf16),
            pltpu.VMEM((2, total, part // 2), bf16),
            pltpu.VMEM((2, SIDE, SIDE, SIDE, 16, columns), bf16),
            pltpu.VMEM((shards, 16, wide), bf16),
            pltpu.VMEM((SIDE, SIDE, 16, layers * adapt), bf16),
            pltpu.VMEM((2, 3, SIDE, 16, half), bf16),
            pltpu.VMEM((2, SIDE, 16, half), bf16),
            pltpu.VMEM((2, 3, 16, half), bf16),
            pltpu.VMEM((SIDE, 2, SIDE, SIDE, 16, layers * adapt), bf16),
            pltpu.VMEM((shards, 16, wide), bf16),
            pltpu.VMEM((layers, 2 * own, wide), f32),
            pltpu.VMEM((layers, 2 * own, wide), f32),
            pltpu.VMEM((2, own, columns), f32),
            pltpu.VMEM((own, columns), f32),
            pltpu.VMEM((16, columns), bf16),
            pltpu.VMEM((3, adapt, part), f32),
            pltpu.VMEM((2, adapt, total), bf16),
            pltpu.VMEM((128, total), f32),
            pltpu.SemaphoreType.DMA((COPIES,)),
            pltpu.SemaphoreType.DMA((COPIES,)),
            pltpu.SemaphoreType.DMA((48,)),
        ],
        compiler_params=pltpu.CompilerParams(
            vmem_limit_bytes=60 * 1024 * 1024, collective_id=0, has_side_effects=True
        ),
        cost_estimate=pl.CostEstimate(
            flops=10**10, bytes_accessed=3 * 10**7, transcendentals=0
        ),
        name="layers",
    )(
        lengths,
        multipliers,
        weight_in[0],
        weight_out[0],
        norm_gain,
        jnp.swapaxes(hidden, 0, 1),
        final_gain[None],
        value_heads,
        response_mask,
        old_values,
        advantages,
    )
    grad_in, grad_out = pl.pallas_call(
        results,
        out_shape=(
            jax.ShapeDtypeStruct(grad_in.shape, f32),
            jax.ShapeDtypeStruct(grad_out.shape, f32),
        ),
        in_specs=[vm, vm],
        out_specs=(vm, vm),
        name="results",
    )(grad_in, grad_out)
    return (grad_in[None], grad_out[None], loss[0, 0])


def solution(mesh):
    return jax.shard_map(
        local,
        mesh=mesh,
        in_specs=(
            P(None, "dp", None),
            P(),
            P(),
            P("section", None),
            P("section", None, None),
            P("section", None, None),
            P(),
            P(),
            P(),
            P(),
            P(),
        ),
        out_specs=(P("section", "dp", None), P("section", None, "dp"), P()),
        check_vma=False,
    )
```
